128 devices in a mesh: row: 8 (over z, core), col: 16 (over y, x).
Axes of the slice: x: 4, y: 4, z: 4, core: 2. Of those that a mesh axis runs over, the one named last changes fastest.
Arguments:
- rest_pos: float32 [3, 262144], P(None, ('row', 'col')), may hold values from 0 to 4
- displacement: float32 [3, 262144], P(None, ('row', 'col')), may hold values from -1.2 to 1.2
- velocity: float32 [3, 262144], P(None, ('row', 'col')), may hold values from -3 to 3
- accel_prev: float32 [3, 262144], P(None, ('row', 'col')), may hold values from -6 to 6
- material: int32 [262144], P(('row', 'col')), may hold values from 0 to 1
- moduli: float32 [2], replicated, may hold values from 0.25 to 4
- pair_owner: int32 [16384], P(('row', 'col')), may hold values from 0 to 255, as said below
- pair_partner: int32 [16384], P(('row', 'col')), may hold values from 0 to 127, as said below
- pair_count: int32 [128], P(('row', 'col')), may hold values from 16 to 128, as said below
- bond_mask: int32 [16384, 128, 128], P(('row', 'col')), may hold values 0 or 1
- broken: int32 [16384, 128, 128], P(('row', 'col')), may hold values 0 or 1
Outputs:
- disp_out: float32 [3, 262144], P(None, ('row', 'col'))
- vel_out: float32 [3, 262144], P(None, ('row', 'col'))
The draws below stay inside these ranges and needn't reach their ends.
Inputs may be any that keep to these rules, and one draw needn't show every extreme that they name: `pair_owner`: on each device the 128 slots name distinct tile pairs; over all devices no two tiles are joined by more than one slot, and no tile is joined with itself. `pair_partner`: drawn together with pair_owner. A device's live slots are its first pair_count slots; the lists and masks of the other slots are to be ignored. Some device has all 128 slots live.
All inputs are finite; a program needn't handle non-finite values. No bound on the sum of `bond_mask` or of `broken` on one device may be relied on, other than what follows from the above.
Results may differ from the reference program's by a relative error of at most 0.00011.
Values sent between devices are 32-bit elements; how exact they have to be, the bound alone decides.
No kernel may reach another device: no remote copies, remote signals or barrier semaphores. Data moves between devices by JAX's collectives and lax.ppermute only.
A program may use at most 64 MiB of HBM per device.

```python
import math
import jax
import jax.numpy as jnp
from jax import lax

TILE = 128
TILE_DEV = 16
STEPS = 2
PAIRS_DEV = 128
PAIRS = 16384
TILES = 2048
POINTS = 262144
ROW_TILES = 256
COL_TILES = 128
N_COL = 16
DEVICES = 128


def pair_combos(key):
    total = ROW_TILES * COL_TILES
    combo = jnp.arange(total, dtype=jnp.int32)
    owner = combo // COL_TILES
    partner = combo % COL_TILES
    device = jnp.arange(DEVICES, dtype=jnp.int32)[:, None]
    first = device // N_COL * ROW_TILES + owner[None, :]
    second = (partner[None, :] // TILE_DEV * N_COL + device % N_COL) * TILE_DEV + partner[None, :] % TILE_DEV
    upward = first < second
    parity = (first + second) % 2 == 1
    valid = (first != second) & (upward != parity)
    noise = jax.random.randint(key, (DEVICES, total), 0, 2 ** 14, dtype=jnp.int32)
    score = noise * total + combo[None, :] + jnp.where(valid, 0, 2 ** 30).astype(jnp.int32)
    chosen = jnp.argsort(score, axis=1)[:, :PAIRS_DEV]
    return (owner[chosen].reshape(-1), partner[chosen].reshape(-1))


def draw_pair_owner(key, part):
    owners, partners = pair_combos(key)
    return owners


def draw_pair_partner(key, part):
    owners, partners = pair_combos(key)
    return partners


def draw_pair_count(key, part):
    key = jax.random.fold_in(key, 7)
    count_key, busy_key = jax.random.split(key)
    lowest = max(1, PAIRS_DEV // 8)
    counts = jax.random.randint(count_key, (DEVICES,), lowest, PAIRS_DEV // 2 + 1, dtype=jnp.int32)
    busiest = jax.random.randint(busy_key, (), 0, DEVICES, dtype=jnp.int32)
    return jnp.where(jnp.arange(DEVICES, dtype=jnp.int32) == busiest, PAIRS_DEV, counts).astype(jnp.int32)


def with_ends(result, stream_key, least, high):
    place = [jax.random.randint(jax.random.fold_in(stream_key, axis), (), 0, length) for axis, length in enumerate(result.shape)]
    widest = result.shape.index(max(result.shape))
    beside = place[:widest] + [(place[widest] + 1) % result.shape[widest]] + place[widest + 1:]
    return result.at[tuple(place)].set(least).at[tuple(beside)].set(high)


def shard_levels(rng, extent, cuts, least, high):
    def one(position, blocks):
        draws = jax.random.uniform(jax.random.fold_in(jax.random.fold_in(rng, 6), position), (blocks,), jnp.float32, least / len(cuts), high / len(cuts))
        return jnp.repeat(jnp.exp(draws), extent[position] // blocks).reshape((-1,) + (1,) * (len(extent) - position - 1))

    gain = one(*cuts[0])
    for cut in cuts[1:]:
        gain = gain * one(*cut)
    return gain


def centred(own_key, shape, scale, most, pieces=(), held_as=jnp.bfloat16):
    array = scale * jax.random.normal(own_key, shape, jnp.float32)
    if pieces:
        array = array * shard_levels(own_key, shape, pieces, -0.22, 0.18)
    return jnp.clip(array, -most, most).astype(held_as)


def setup_inputs(seed: int = 0) -> dict:
    key_list = jax.random.split(jax.random.key(seed), 12)
    return {
        "rest_pos": jnp.clip(4.0 * jax.random.uniform(key_list[0], (3, POINTS), jnp.float32) ** shard_levels(key_list[0], (3, POINTS), ((1, 128),), -0.2, 0.2), 0.0, 4.0),
        "displacement": centred(key_list[1], (3, POINTS), 0.3, 1.2, ((1, 128),), jnp.float32),
        "velocity": centred(key_list[2], (3, POINTS), 0.5, 3.0, ((1, 128),), jnp.float32),
        "accel_prev": centred(key_list[3], (3, POINTS), 1.0, 6.0, ((1, 128),), jnp.float32),
        "material": with_ends(jax.random.randint(key_list[4], (POINTS,), 0, 2), jax.random.fold_in(key_list[4], 1), 0, 1).astype(jnp.int32),
        "moduli": jnp.clip(jnp.exp(jax.random.uniform(key_list[5], (2,), jnp.float32, math.log(0.25), math.log(4.0))), 0.25, 4.0),
        "pair_owner": draw_pair_owner(jax.random.fold_in(key_list[11], 71), 0),
        "pair_partner": draw_pair_partner(jax.random.fold_in(key_list[11], 71), 0),
        "pair_count": draw_pair_count(jax.random.fold_in(key_list[11], 71), 0),
        "bond_mask": with_ends((jax.random.randint(key_list[9], (PAIRS, TILE, TILE), 0, 4) < 3).astype(jnp.int32), jax.random.fold_in(key_list[9], 1), 0, 1),
        "broken": with_ends((jax.random.randint(key_list[10], (PAIRS, TILE, TILE), 0, 5) < 1).astype(jnp.int32), jax.random.fold_in(key_list[10], 1), 0, 1),
    }


RADIUS = 1.0
TIME_STEP = 0.5
FIBER_GAIN = 8.0
BLOCK_PAIRS = 8

def bond_terms(owners, others, weight, strength):
    rest_vec = [others[component][:, None, :] - owners[component][:, :, None] for component in range(3)]
    current = [rest_vec[component] + others[component + 3][:, None, :] - owners[component + 3][:, :, None] for component in range(3)]
    rest_len = jnp.sqrt(rest_vec[0] * rest_vec[0] + rest_vec[1] * rest_vec[1] + rest_vec[2] * rest_vec[2] + RADIUS * RADIUS)
    cur_len = jnp.sqrt(current[0] * current[0] + current[1] * current[1] + current[2] * current[2] + RADIUS * RADIUS)
    stretch = (cur_len - rest_len) / rest_len
    axial_cos = rest_vec[0] / rest_len
    stiffness = jnp.sqrt(owners[6][:, :, None] * others[6][:, None, :]) * (1.0 + FIBER_GAIN * owners[7][:, :, None] * others[7][:, None, :] * axial_cos * axial_cos)
    factor = strength * weight * stiffness * stretch / cur_len
    on_owner = jnp.stack([lax.optimization_barrier(jnp.sum(factor * current[component], axis=2)) for component in range(3)])
    on_partner = jnp.stack([-lax.optimization_barrier(jnp.sum(factor * current[component], axis=1)) for component in range(3)])
    return (on_owner, on_partner)

def all_forces(state_rows, owner_tiles, partner_tiles, active, bond_mask, broken, strength):
    summed = jnp.zeros((3, TILES, TILE), jnp.float32)

    def cross(summed, block_id):
        first_slot = block_id * BLOCK_PAIRS
        owner_ids = lax.dynamic_slice_in_dim(owner_tiles, first_slot, BLOCK_PAIRS)
        partner_ids = lax.dynamic_slice_in_dim(partner_tiles, first_slot, BLOCK_PAIRS)
        live_part = lax.dynamic_slice_in_dim(active, first_slot, BLOCK_PAIRS)
        bonds = lax.dynamic_slice_in_dim(bond_mask, first_slot, BLOCK_PAIRS)
        cracks = lax.dynamic_slice_in_dim(broken, first_slot, BLOCK_PAIRS)
        weight = (bonds * (1 - cracks) * live_part[:, None, None]).astype(jnp.float32)
        on_owner, on_partner = bond_terms(state_rows[:, owner_ids], state_rows[:, partner_ids], weight, strength)
        summed = summed.at[:, owner_ids].add(on_owner)
        summed = summed.at[:, partner_ids].add(on_partner)
        return (summed, None)
    summed, unused = lax.scan(cross, summed, jnp.arange(PAIRS // BLOCK_PAIRS, dtype=jnp.int32))

    def inner(summed, block_id):
        first_slot = block_id * BLOCK_PAIRS
        tile_set = lax.dynamic_slice_in_dim(state_rows, first_slot, BLOCK_PAIRS, 1)
        weight = jnp.ones((BLOCK_PAIRS, TILE, TILE), jnp.float32)
        on_owner, unused_part = bond_terms(tile_set, tile_set, weight, strength)
        updated = lax.dynamic_slice_in_dim(summed, first_slot, BLOCK_PAIRS, 1) + on_owner
        return (lax.dynamic_update_slice_in_dim(summed, updated, first_slot, 1), None)
    summed, unused = lax.scan(inner, summed, jnp.arange(TILES // BLOCK_PAIRS, dtype=jnp.int32))
    return summed

def reference(rest_pos, displacement, velocity, accel_prev, material, moduli, pair_owner, pair_partner, pair_count, bond_mask, broken):
    strength = 1.5 / math.sqrt(TILE * (1.0 + PAIRS_DEV / TILE_DEV))
    fibrous = material.astype(jnp.float32)
    modulus = jnp.where(material == 1, moduli[1], moduli[0])
    device = jnp.arange(PAIRS, dtype=jnp.int32) // PAIRS_DEV
    slot_ids = jnp.arange(PAIRS, dtype=jnp.int32) % PAIRS_DEV
    owner_tiles = device // N_COL * ROW_TILES + pair_owner
    partner_tiles = (pair_partner // TILE_DEV * N_COL + device % N_COL) * TILE_DEV + pair_partner % TILE_DEV
    active = (slot_ids < pair_count[device]).astype(jnp.int32)
    displaced = displacement
    moving = velocity
    acceleration = accel_prev
    for step_id in range(STEPS):
        moving = moving + 0.5 * TIME_STEP * acceleration
        displaced = displaced + TIME_STEP * moving
        state_rows = jnp.concatenate([rest_pos, displaced, modulus[None], fibrous[None]], 0).reshape(8, TILES, TILE)
        acceleration = all_forces(state_rows, owner_tiles, partner_tiles, active, bond_mask, broken, strength).reshape(3, POINTS)
        moving = moving + 0.5 * TIME_STEP * acceleration
    return (displaced, moving)
```

```python
import math, functools
import jax, jax.numpy as jnp
from jax import lax
from jax.sharding import PartitionSpec as P
from jax.experimental import pallas as pl
from jax.experimental.pallas import tpu as pltpu

TILE=128
STRENGTH=1.5/math.sqrt(128*9.0)

def rows_iota(n=8):
    return lax.broadcasted_iota(jnp.int32,(n,TILE),0)

def split3(c):
    c1=c.astype(jnp.bfloat16).astype(jnp.float32)
    r=c-c1
    c2=r.astype(jnp.bfloat16).astype(jnp.float32)
    return c1,c2,r-c2

def split2(c):
    c1=c.astype(jnp.bfloat16).astype(jnp.float32)
    return c1,c-c1

def features(s):
    r=rows_iota()
    f=jnp.broadcast_to(s[7:8],(8,TILE)); x=jnp.broadcast_to(s[4:5],(8,TILE)); m=jnp.broadcast_to(s[3:4],(8,TILE))
    c=jnp.where(r==3,f*x,s)
    sq=c*c
    v=sq+pltpu.roll(sq,7,0)+pltpu.roll(sq,6,0)
    w=jnp.where(r==3,sq,v+0.5)
    ones=jnp.where(r==3,f,1.0)
    z=m*jnp.where(r==3,1.0,s)
    z1,z2=split2(z)
    zz=jnp.where(r<4,z1,pltpu.roll(z2,4,0))
    zz=jnp.concatenate([zz,jnp.zeros_like(zz)],0).astype(jnp.bfloat16)
    return split3(c),split3(w),ones,zz,m

def patterns():
    blk=lax.broadcasted_iota(jnp.int32,(96,TILE),0)//8
    row=lax.broadcasted_iota(jnp.int32,(96,TILE),0)%8
    coord=blk<6
    out=[]
    for lo,hi,norm,scale in ((0,3,0,1.0),(4,7,4,1.0),(3,4,3,8.0)):
        a=jnp.where((row>=lo)&(row<hi),-2.0*scale,0.0)
        b=jnp.where(row==norm,scale,0.0)
        out.append(jnp.where(coord,a,b))
    return out

def post(acc,s,m):
    t=acc[:8]
    t=t+pltpu.roll(t,4,0)
    sw=jnp.broadcast_to(t[3:4],(8,TILE))
    return (STRENGTH*m)*(t-s*sw)

def bond(so,sp,fo,fp,pat_ref,word,both):
    (c1,c2,c3),(w1,w2,w3),one,zo,mo=fo
    (d1,d2,d3),(x1,x2,x3),onep,zp,mp=fp
    left=jnp.concatenate([c1,c1,c2,c2,c1,c3,w1,w2,w3,one,one,one],0).astype(jnp.bfloat16)
    base=jnp.concatenate([d1,d2,d1,d2,d3,d1,onep,onep,onep,x1,x2,x3],0).astype(jnp.bfloat16)
    right=jnp.concatenate([base*pat_ref[0],base*pat_ref[1],base*pat_ref[2]],1)
    d=lax.dot_general(left,right,(((0,),(0,)),((),())),preferred_element_type=jnp.float32)
    il=lax.rsqrt(jnp.maximum(d[:,:TILE],1.0))
    iL=lax.rsqrt(d[:,TILE:2*TILE])
    w=(iL-il)*(1.0+d[:,2*TILE:]*(iL*iL))
    if word is not None:
        w=jnp.concatenate([jnp.where((word&(1<<k))!=0,w[8*k:8*k+8],0.0) for k in range(16)],0)
    wh=w.astype(jnp.bfloat16)
    wl=(w-wh.astype(jnp.float32)).astype(jnp.bfloat16)
    nt=(((1,),(1,)),((),()))
    ao=lax.dot_general(zp,wh,nt,preferred_element_type=jnp.float32)+lax.dot_general(zp,wl,nt,preferred_element_type=jnp.float32)
    on_o=post(ao,so,mo)
    if not both: return on_o,None
    ap=jnp.dot(zo,wh,preferred_element_type=jnp.float32)+jnp.dot(zo,wl,preferred_element_type=jnp.float32)
    return on_o,post(ap,sp,mp)

def pair_kernel(n_col,n_row,unroll,own_ref,count_ref,owner_ref,partner_ref,row_ref,col_ref,packed_ref,rowf_ref,colf_ref,pat_ref):
    for k,p in enumerate(patterns()):
        pat_ref[k]=p.astype(jnp.bfloat16)
    rowf_ref[...]=jnp.zeros_like(rowf_ref)
    colf_ref[...]=jnp.zeros_like(colf_ref)
    live=count_ref[0]
    def load(ref,t):
        return ref[pl.ds((t//16)*128+t%16,8,stride=16),:]
    def add(ref,t,val):
        at=pl.ds((t//16)*48+t%16,3,stride=16)
        ref[at,:]=ref[at,:]+val[:3]
    def own_body(i,c):
        base=own_ref[0]*16
        res=[]
        for j in range(unroll):
            t=base+i*unroll+j
            s=load(row_ref,t)
            f=features(s)
            res.append((t,bond(s,s,f,f,pat_ref,None,False)[0]))
        for t,v in res: add(rowf_ref,t,v)
        return c
    lax.fori_loop(0,16//unroll,own_body,0)
    def body(i,c):
        res=[]
        for j in range(unroll):
            slot=i*unroll+j
            o=owner_ref[slot]; p=partner_ref[slot]
            so=load(row_ref,o); sp=load(col_ref,p)
            alive=jnp.where(slot<live,-1,0)
            word=packed_ref[slot]&alive
            a,b=bond(so,sp,features(so),features(sp),pat_ref,word,True)
            res.append((o,p,a,b))
        for o,p,a,b in res:
            add(rowf_ref,o,a); add(colf_ref,p,b)
        return c
    lax.fori_loop(0,(live+unroll-1)//unroll,body,0)

def pair_forces(own,count,owner,partner,row,col,packed,unroll=4):
    n_col=row.shape[0]//128; n_row=col.shape[0]//128
    smem=pl.BlockSpec(memory_space=pltpu.SMEM); vmem=pl.BlockSpec(memory_space=pltpu.VMEM)
    return pl.pallas_call(functools.partial(pair_kernel,n_col,n_row,unroll),
        out_shape=(jax.ShapeDtypeStruct((n_col*48,TILE),jnp.float32),jax.ShapeDtypeStruct((n_row*48,TILE),jnp.float32)),
        in_specs=[smem]*4+[vmem]*3,out_specs=(vmem,vmem),
        scratch_shapes=[pltpu.VMEM((3,96,TILE),jnp.bfloat16)],
        compiler_params=pltpu.CompilerParams(vmem_limit_bytes=48*2**20),
        name="pair_forces")(own,count,owner,partner,row,col,packed)

def pack_kernel(count_ref,bond_ref,broken_ref,out_ref):
    i=pl.program_id(0)
    @pl.when(i*8<count_ref[0])
    def _():
        for j in range(8):
            acc=None
            for k in range(16):
                b=bond_ref[j,8*k:8*k+8,:]; c=broken_ref[j,8*k:8*k+8,:]
                t=(b&(1-c))<<k
                acc=t if acc is None else acc|t
            out_ref[j]=acc

def pack(count,bond_mask,broken):
    n=bond_mask.shape[0]
    def idx(i,cnt): return (jnp.minimum(i,(cnt[0]+7)//8-1),0,0)
    return pl.pallas_call(pack_kernel,
        grid_spec=pltpu.PrefetchScalarGridSpec(num_scalar_prefetch=1,grid=(n//8,),
            in_specs=[pl.BlockSpec((8,TILE,TILE),idx)]*2,out_specs=pl.BlockSpec((8,8,TILE),idx)),
        out_shape=jax.ShapeDtypeStruct((n,8,TILE),jnp.int32),
        compiler_params=pltpu.CompilerParams(vmem_limit_bytes=48*2**20),
        name="pack_bonds")(count,bond_mask,broken)


STEPS=2
TIME_STEP=0.5


def spread(block, axis, n):
    return lax.all_to_all(jnp.broadcast_to(block[None],(n,)+block.shape),axis,0,0,tiled=True)


def gather_sum(parts, axis):
    return jnp.sum(lax.all_to_all(parts,axis,0,0,tiled=True),axis=0)


def per_device(rest_pos, displacement, velocity, accel_prev, material, moduli, pair_owner, pair_partner, pair_count, bond_mask, broken):
    n_row=lax.axis_size("row"); n_col=lax.axis_size("col")
    tiles=material.shape[0]//TILE
    shape=(3,tiles,TILE)
    rest=rest_pos.reshape(shape)-2.0
    u=displacement.reshape(shape); v=velocity.reshape(shape); a=accel_prev.reshape(shape)
    fibrous=material.reshape(1,tiles,TILE).astype(jnp.float32)
    root=jnp.sqrt(moduli)
    root=jnp.where(material.reshape(1,tiles,TILE)==1,root[1],root[0])
    own=lax.axis_index("col").reshape(1).astype(jnp.int32)
    packed=pack(pair_count,bond_mask,broken)
    fixed_row=fixed_col=None
    for step in range(STEPS):
        v=v+0.5*TIME_STEP*a
        u=u+TIME_STEP*v
        if step==0:
            state=jnp.concatenate([rest+u,root,rest,fibrous],0)
            row=spread(state,"col",n_col); col=spread(state,"row",n_row)
        else:
            row=jnp.concatenate([spread(rest+u,"col",n_col),row[:,3:]],1)
            col=jnp.concatenate([spread(rest+u,"row",n_row),col[:,3:]],1)
        rowf,colf=pair_forces(own,pair_count,pair_owner,pair_partner,row.reshape(-1,TILE),col.reshape(-1,TILE),packed,8)
        a=(gather_sum(rowf.reshape((n_col,)+shape),"col")+gather_sum(colf.reshape((n_row,)+shape),"row"))
        v=v+0.5*TIME_STEP*a
    return u.reshape(3,-1),v.reshape(3,-1)


def solution(mesh):
    points=P(None,("row","col")); flat=P(("row","col")); masks=P(("row","col"),None,None)
    return jax.shard_map(per_device,mesh=mesh,in_specs=(points,)*4+(flat,P())+(flat,)*3+(masks,)*2,out_specs=(points,points),check_vma=False)
```

```python
import functools
import math

import jax
import jax.numpy as jnp
from jax import lax
from jax.experimental import pallas as pl
from jax.experimental.pallas import tpu as pltpu
from jax.sharding import PartitionSpec as P

TILE = 128
TILE_DEV = 16
PAIRS_DEV = 128
STEPS = 2
TIME_STEP = 0.5
CENTRE = 2.0
STRENGTH = 1.5 / math.sqrt(TILE * (1.0 + PAIRS_DEV / TILE_DEV))
UNROLL = 16
CORES = 2
PACK = 16
LIMIT = 48 * 2**20
VMEM = pl.BlockSpec(memory_space=pltpu.VMEM)
SMEM = pl.BlockSpec(memory_space=pltpu.SMEM)


def f32(*shape):
    return jax.ShapeDtypeStruct(shape, jnp.float32)


def rows_iota(n=8):
    return lax.broadcasted_iota(jnp.int32,(n,TILE),0)

def halves(c):
    c1=c.astype(jnp.bfloat16).astype(jnp.float32)
    return c1,(c-c1).astype(jnp.bfloat16).astype(jnp.float32)

def thirds(c):
    c1,c2=halves(c)
    return c1,c2,(c-c1)-c2

def row_of(s,k):
    return jnp.broadcast_to(s[k:k+1],(8,TILE))

def features(s,owner,alive=None):
    r=rows_iota()
    f=row_of(s,7); m=row_of(s,3)
    if alive is not None:
        m=m*alive
    c1,c2=halves(jnp.where(r==3,f*row_of(s,4),s))
    c=c1+c2
    sq=c*c
    w=jnp.where(r==3,sq,sq+pltpu.roll(sq,7,0)+pltpu.roll(sq,6,0)+0.5)
    z1,z2=halves(m*jnp.where(r==3,1.0,s))
    z=jnp.where(r<4,z1,pltpu.roll(z2,4,0))
    z=jnp.concatenate([z,jnp.zeros_like(z)],0).astype(jnp.bfloat16)
    if owner:
        ones=jnp.where(r==5,f,1.0)
        n=[jnp.where((r==0)|(r==3)|(r==4),t,ones) for t in thirds(w)]
        x=[c1,c1,c2,c2]+n+[jnp.zeros_like(ones)]
    else:
        ones=jnp.where(r==3,f,1.0)
        n=[jnp.where((r==2)|(r==5)|(r==6),t,ones) for t in thirds(pltpu.roll(w,2,0))]
        x=[c1,c2,c1,c2]+n+[jnp.zeros_like(ones)]
    return jnp.concatenate(x,0).astype(jnp.bfloat16),z,m

def patterns():
    row=lax.broadcasted_iota(jnp.int32,(64,TILE),0)
    coord=row<32; spare=row>=56
    row=row%8
    def pick(lo,hi,n1,n2,scale):
        c=jnp.where((row>=lo)&(row<hi),-2.0*scale,0.0)
        n=jnp.where((row==n1)|(row==n2),scale,0.0)
        return jnp.where(spare,0.0,jnp.where(coord,c,n))
    now=pick(0,3,0,2,1.0); rest=pick(4,7,4,6,1.0)
    return now,rest,rest+pick(3,4,3,5,8.0)

def post(acc,s,m):
    t=acc[:8,:TILE]+acc[:8,TILE:]
    t=t+pltpu.roll(t,4,0)
    return (STRENGTH*m)*(t-s*row_of(t,3))

def lengths(left,base,pat_ref):
    right=jnp.concatenate([base*pat_ref[0],base*pat_ref[1],base*pat_ref[2]],1)
    return lax.dot_general(left,right,(((0,),(0,)),((),())),preferred_element_type=jnp.float32)

def weights(d,mask):
    il=lax.rsqrt(jnp.maximum(d[:,:TILE],1.0))
    iL=lax.rsqrt(d[:,TILE:2*TILE])
    w=(iL-il)*(d[:,2*TILE:]*(iL*iL))
    wh=w.astype(jnp.bfloat16)
    wl=(w-wh.astype(jnp.float32)).astype(jnp.bfloat16)
    if mask is not None:
        wh=wh*mask; wl=wl*mask
    return wh,wl

def sum_owner(z,w):
    return lax.dot_general(z,jnp.concatenate(w,0),(((1,),(1,)),((),())),preferred_element_type=jnp.float32)

def sum_partner(z,w):
    return jnp.dot(z,jnp.concatenate(w,1),preferred_element_type=jnp.float32)

def pack_kernel(count_ref,bond_ref,broken_ref,out_ref):
    i=pl.program_id(0)
    @pl.when(i*PACK<count_ref[0])
    def _():
        out_ref[...]=(bond_ref[...]*(1-broken_ref[...])).astype(jnp.float32).astype(jnp.bfloat16)

def pack(count,bond_mask,broken):
    n=bond_mask.shape[0]
    def idx(i,cnt): return (jnp.minimum(i,(cnt[0]+PACK-1)//PACK-1),0,0)
    return pl.pallas_call(pack_kernel,
        grid_spec=pltpu.PrefetchScalarGridSpec(num_scalar_prefetch=1,grid=(n//PACK,),
            in_specs=[pl.BlockSpec((PACK,TILE,TILE),idx)]*2,out_specs=pl.BlockSpec((PACK,TILE,TILE),idx)),
        out_shape=jax.ShapeDtypeStruct((n,TILE,TILE),jnp.bfloat16),
        compiler_params=pltpu.CompilerParams(vmem_limit_bytes=LIMIT),
        name="pack_bonds")(count,bond_mask,broken)

def pair_kernel(n_z, fresh, *refs):
    count_ref, owner_ref, partner_ref, mask_ref, row_ref = refs[:5]
    col_refs = refs[5:5 + n_z]
    at = 5 + n_z
    now_row_ref, now_col_refs = None, None
    if not fresh:
        now_row_ref = refs[at]
        now_col_refs = refs[at + 1:at + 1 + n_z]
        at += 1 + n_z
    rowf_ref, mine_ref, sibling_ref, pat_ref, rows_ref, cols_ref, colf_ref = refs[at:]
    n_col = row_ref.shape[0]
    full = 8 * TILE_DEV
    part = 3 * TILE_DEV
    at_row = lax.axis_index("row")
    z, core = at_row // CORES, at_row % CORES
    for k, p in enumerate(patterns()):
        pat_ref[k] = p.astype(jnp.bfloat16)
    rowf_ref[...] = jnp.zeros_like(rowf_ref)
    colf_ref[...] = jnp.zeros_like(colf_ref)
    for c in range(n_col):
        rows_ref[c * full:(c + 1) * full] = row_ref[c].reshape(full, TILE)
        if not fresh:
            rows_ref[c * full:c * full + part] = now_row_ref[c].reshape(part, TILE)
    for d in range(n_z):
        src = (z + n_z - d) % n_z
        for j in range(CORES):
            r = src * CORES + (core if j == 0 else 1 - core)
            start = pl.multiple_of(r * full, full)
            cols_ref[pl.ds(start, full)] = col_refs[d][j].reshape(full, TILE)
            if not fresh:
                cols_ref[pl.ds(start, part)] = now_col_refs[d][j].reshape(part, TILE)
    live = count_ref[0]

    def load(ref, t):
        return ref[pl.ds((t // TILE_DEV) * full + t % TILE_DEV, 8, stride=TILE_DEV), :]

    def add(ref, t, val):
        where = pl.ds((t // TILE_DEV) * part + t % TILE_DEV, 3, stride=TILE_DEV)
        ref[where, :] = ref[where, :] + val[:3]

    def run(slots, masks, both):
        d = [lengths(fo[0], fp[0], pat_ref) for _, _, _, _, fo, fp in slots]
        w = [weights(x, m) for x, m in zip(d, masks)]
        ao = [sum_owner(q[5][1], x) for q, x in zip(slots, w)]
        ap = [sum_partner(q[4][1], x) for q, x in zip(slots, w)] if both else None
        for j, (o, p, so, sp, fo, fp) in enumerate(slots):
            add(rowf_ref, o, post(ao[j], so, fo[2]))
            if both:
                add(colf_ref, p, post(ap[j], sp, fp[2]))

    own = []
    for j in range(TILE_DEV):
        t = lax.axis_index("col") * TILE_DEV + j
        s = load(rows_ref, t)
        own.append((t, t, s, s, features(s, True), features(s, False)))
    run(own, [None] * TILE_DEV, False)

    def body(i, carry):
        slots = []
        masks = []
        for j in range(UNROLL):
            slot = i * UNROLL + j
            o = owner_ref[slot]
            p = partner_ref[slot]
            so = load(rows_ref, o)
            sp = load(cols_ref, p)
            alive = jnp.where(slot < live, 1.0, 0.0)
            slots.append((o, p, so, sp, features(so, True, alive), features(sp, False, alive)))
            masks.append(mask_ref[slot])
        run(slots, masks, True)
        return carry

    lax.fori_loop(0, (live + UNROLL - 1) // UNROLL, body, 0)
    for i in range(n_z):
        for ref, c in ((mine_ref, core), (sibling_ref, 1 - core)):
            start = pl.multiple_of((i * CORES + c) * part, part)
            ref[i] = colf_ref[pl.ds(start, part)].reshape(3, TILE_DEV, TILE)


def pair_forces(count, owner, partner, masks, row, cols, now_row=None, now_cols=()):
    n_col, n_z = row.shape[0], len(cols)
    fresh = now_row is None
    more = () if fresh else (now_row, *now_cols)
    shares = f32(n_z, 3, TILE_DEV, TILE)
    return pl.pallas_call(
        functools.partial(pair_kernel, n_z, fresh),
        out_shape=(f32(n_col * 3 * TILE_DEV, TILE), shares, shares),
        in_specs=[SMEM] * 3 + [VMEM] * (2 + n_z + len(more)),
        out_specs=(VMEM,) * 3,
        scratch_shapes=[
            pltpu.VMEM((3, 64, TILE), jnp.bfloat16),
            pltpu.VMEM((n_col * 8 * TILE_DEV, TILE), jnp.float32),
            pltpu.VMEM((n_z * CORES * 8 * TILE_DEV, TILE), jnp.float32),
            pltpu.VMEM((n_z * CORES * 3 * TILE_DEV, TILE), jnp.float32),
        ],
        compiler_params=pltpu.CompilerParams(vmem_limit_bytes=LIMIT),
        name="pair_forces",
    )(count, owner, partner, masks, row, *cols, *more)


def start_kernel(moduli_ref, material_ref, rest_ref, disp_ref, vel_ref, acc_ref, spread_ref, state_ref, u_ref, v_ref):
    for c in range(3):
        for t in range(TILE_DEV):
            lanes = pl.ds(t * TILE, TILE)
            v = vel_ref[c:c + 1, lanes] + 0.5 * TIME_STEP * acc_ref[c:c + 1, lanes]
            u = disp_ref[c:c + 1, lanes] + TIME_STEP * v
            x = rest_ref[c:c + 1, lanes] - CENTRE
            v_ref[c, t:t + 1, :] = v
            u_ref[c, t:t + 1, :] = u
            state_ref[c, t:t + 1, :] = x + u
            state_ref[4 + c, t:t + 1, :] = x
    fibre = material_ref[...] == 1
    modulus = jnp.where(fibre, moduli_ref[1], moduli_ref[0])
    state_ref[3] = jnp.sqrt(modulus)
    state_ref[7] = jnp.where(fibre, 1.0, 0.0)
    for i in range(spread_ref.shape[0]):
        spread_ref[i] = state_ref[...]


def start(n_col, moduli, material, rest, disp, vel, acc):
    block = (3, TILE_DEV, TILE)
    return pl.pallas_call(
        start_kernel,
        out_shape=(f32(n_col, 8, TILE_DEV, TILE), f32(8, TILE_DEV, TILE), f32(*block), f32(*block)),
        in_specs=[SMEM] + [VMEM] * 5,
        out_specs=(VMEM,) * 4,
        name="first_half_step",
    )(moduli, material, rest, disp, vel, acc)


def share_kernel(mine_ref, other_ref, *out_refs):
    n_z = len(out_refs)
    z = lax.axis_index("row") // CORES
    for d, out_ref in enumerate(out_refs):
        at = (z + d) % n_z
        out_ref[...] = mine_ref[at] + other_ref[at]


def shares(mine, other):
    n_z = mine.shape[0]
    return pl.pallas_call(
        share_kernel,
        out_shape=(f32(*mine.shape[1:]),) * n_z,
        in_specs=[VMEM] * 2,
        out_specs=(VMEM,) * n_z,
        name="column_shares",
    )(mine, other)


def total(row_ref, col_refs):
    force = row_ref[0]
    for i in range(1, row_ref.shape[0]):
        force = force + row_ref[i]
    for ref in col_refs:
        force = force + ref[...]
    return force


def step_kernel(n_z, row_ref, *refs):
    col_refs = refs[:n_z]
    state_ref, u_ref, v_ref, spread_ref, now_ref, new_u_ref, new_v_ref = refs[n_z:]
    force = total(row_ref, col_refs)
    v = v_ref[...] + TIME_STEP * force
    u = u_ref[...] + TIME_STEP * v
    now = state_ref[4:7] + u
    new_u_ref[...] = u
    new_v_ref[...] = v
    now_ref[...] = now
    for i in range(spread_ref.shape[0]):
        spread_ref[i] = now


def next_step(row, cols, state, u, v):
    return pl.pallas_call(
        functools.partial(step_kernel, len(cols)),
        out_shape=(f32(*row.shape),) + (f32(*u.shape),) * 3,
        in_specs=[VMEM] * (4 + len(cols)),
        out_specs=(VMEM,) * 4,
        name="next_step",
    )(row, *cols, state, u, v)


def last_kernel(n_z, row_ref, *refs):
    col_refs = refs[:n_z]
    u_ref, v_ref, disp_ref, vel_ref = refs[n_z:]
    v = v_ref[...] + 0.5 * TIME_STEP * total(row_ref, col_refs)
    for c in range(3):
        for t in range(TILE_DEV):
            lanes = pl.ds(t * TILE, TILE)
            disp_ref[c:c + 1, lanes] = u_ref[c, t:t + 1, :]
            vel_ref[c:c + 1, lanes] = v[c, t:t + 1, :]


def last_step(row, cols, u, v):
    points = f32(3, TILE_DEV * TILE)
    return pl.pallas_call(
        functools.partial(last_kernel, len(cols)),
        out_shape=(points, points),
        in_specs=[VMEM] * (3 + len(cols)),
        out_specs=(VMEM,) * 2,
        name="last_half_step",
    )(row, *cols, u, v)


def to_sibling(x, n_row):
    return lax.ppermute(x, "row", [(i, i ^ 1) for i in range(n_row)])


def along_z(x, d, n_row):
    n_z = n_row // CORES
    return lax.ppermute(x, "row", [(i, (i // CORES + d) % n_z * CORES + i % CORES) for i in range(n_row)])


def swap(x):
    return lax.all_to_all(x, "col", 0, 0, tiled=True)


def column_gather(block, n_row):
    both = jnp.stack([block, to_sibling(block, n_row)])
    return [both] + [along_z(both, d, n_row) for d in range(1, n_row // CORES)]


def column_sum(mine, sibling, n_row):
    parts = shares(mine, to_sibling(sibling, n_row))
    return [parts[0]] + [along_z(parts[d], d, n_row) for d in range(1, n_row // CORES)]


def per_device(
    rest_pos, displacement, velocity, accel_prev, material, moduli, pair_owner, pair_partner, pair_count, bond_mask, broken
):
    n_row, n_col = lax.axis_size("row"), lax.axis_size("col")
    spread, state, u, v = start(
        n_col, moduli, material.reshape(TILE_DEV, TILE), rest_pos, displacement, velocity, accel_prev
    )
    row = swap(spread)
    cols = column_gather(state, n_row)
    masks = pack(pair_count, bond_mask, broken)
    now = ()
    for step in range(STEPS):
        rowf, mine, sibling = pair_forces(pair_count, pair_owner, pair_partner, masks, row, cols, *now)
        row_part = swap(rowf.reshape(n_col, 3, TILE_DEV, TILE))
        col_part = column_sum(mine, sibling, n_row)
        if step < STEPS - 1:
            spread, block, u, v = next_step(row_part, col_part, state, u, v)
            now = (swap(spread), column_gather(block, n_row))
    return last_step(row_part, col_part, u, v)


def solution(mesh):
    points, flat, masks = P(None, ("row", "col")), P(("row", "col")), P(("row", "col"), None, None)
    return jax.shard_map(
        per_device,
        mesh=mesh,
        in_specs=(points,) * 4 + (flat, P()) + (flat,) * 3 + (masks,) * 2,
        out_specs=(points, points),
        check_vma=False,
    )
```

```python
import functools
import math

import jax
import jax.numpy as jnp
from jax import lax
from jax.experimental import pallas as pl
from jax.experimental.pallas import tpu as pltpu
from jax.sharding import PartitionSpec as P

TILE = 128
TILE_DEV = 16
PAIRS_DEV = 128
STEPS = 2
TIME_STEP = 0.5
CENTRE = 2.0
STRENGTH = 1.5 / math.sqrt(TILE * (1.0 + PAIRS_DEV / TILE_DEV))
UNROLL = 16
LEAD = 4
CORES = 2
LIMIT = int(52 * 2**20)
SMALL = 4 * 2**20
VMEM = pl.BlockSpec(memory_space=pltpu.VMEM)
ANY = pl.BlockSpec(memory_space=pltpu.HBM)
SMEM = pl.BlockSpec(memory_space=pltpu.SMEM)


def f32(*shape):
    return jax.ShapeDtypeStruct(shape, jnp.float32)


def rows_iota(n=8):
    return lax.broadcasted_iota(jnp.int32,(n,TILE),0)

def halves(c):
    c1=c.astype(jnp.bfloat16).astype(jnp.float32)
    return c1,(c-c1).astype(jnp.bfloat16).astype(jnp.float32)

def thirds(c):
    c1,c2=halves(c)
    return c1,c2,(c-c1)-c2

def row_of(s,k):
    return jnp.broadcast_to(s[k:k+1],(8,TILE))

def features(s,owner,alive=None):
    r=rows_iota()
    f=row_of(s,7); m=row_of(s,3)
    if alive is not None:
        m=m*alive
    c1,c2=halves(jnp.where(r==3,f*row_of(s,4),s))
    c=c1+c2
    sq=c*c
    w=jnp.where(r==3,sq,sq+pltpu.roll(sq,7,0)+pltpu.roll(sq,6,0)+0.5)
    z1,z2=halves(m*jnp.where(r==3,1.0,s))
    z=jnp.where(r<4,z1,pltpu.roll(z2,4,0))
    z=jnp.concatenate([z,jnp.zeros_like(z)],0).astype(jnp.bfloat16)
    if owner:
        ones=jnp.where(r==5,f,1.0)
        n=[jnp.where((r==0)|(r==3)|(r==4),t,ones) for t in thirds(w)]
        x=[c1,c1,c2,c2]+n+[jnp.zeros_like(ones)]
    else:
        ones=jnp.where(r==3,f,1.0)
        n=[jnp.where((r==2)|(r==5)|(r==6),t,ones) for t in thirds(pltpu.roll(w,2,0))]
        x=[c1,c2,c1,c2]+n+[jnp.zeros_like(ones)]
    return jnp.concatenate(x,0).astype(jnp.bfloat16),z,m

def patterns():
    row=lax.broadcasted_iota(jnp.int32,(64,TILE),0)
    coord=row<32; spare=row>=56
    row=row%8
    def pick(lo,hi,n1,n2,scale):
        c=jnp.where((row>=lo)&(row<hi),-2.0*scale,0.0)
        n=jnp.where((row==n1)|(row==n2),scale,0.0)
        return jnp.where(spare,0.0,jnp.where(coord,c,n))
    now=pick(0,3,0,2,1.0); rest=pick(4,7,4,6,1.0)
    return now,rest,rest+pick(3,4,3,5,8.0)

def post(acc,s,m):
    t=acc[:8,:TILE]+acc[:8,TILE:]
    t=t+pltpu.roll(t,4,0)
    return (STRENGTH*m)*(t-s*row_of(t,3))

def lengths(left,base,pat_ref):
    right=jnp.concatenate([base*pat_ref[0],base*pat_ref[1],base*pat_ref[2]],1)
    return lax.dot_general(left,right,(((0,),(0,)),((),())),preferred_element_type=jnp.float32)

def weights(d,mask):
    il=lax.rsqrt(jnp.maximum(d[:,:TILE],1.0))
    iL=lax.rsqrt(d[:,TILE:2*TILE])
    t=iL-il
    if mask is not None:
        t=jnp.where(mask[0]>mask[1],t,0.0)
    w=t*(d[:,2*TILE:]*(iL*iL))
    wh=w.astype(jnp.bfloat16)
    wl=(w-wh.astype(jnp.float32)).astype(jnp.bfloat16)
    return wh,wl

def sum_owner(z,w):
    return lax.dot_general(z,jnp.concatenate(w,0),(((1,),(1,)),((),())),preferred_element_type=jnp.float32)

def sum_partner(z,w):
    return jnp.dot(z,jnp.concatenate(w,1),preferred_element_type=jnp.float32)

def pair_kernel(n_z, fresh, *refs):
    count_ref, owner_ref, partner_ref, bond_ref, broken_ref, row_ref = refs[:6]
    col_refs = refs[6:6 + n_z]
    at = 6 + n_z
    now_row_ref, now_col_refs = None, None
    if not fresh:
        now_row_ref = refs[at]
        now_col_refs = refs[at + 1:at + 1 + n_z]
        at += 1 + n_z
    rowf_ref, mine_ref, sibling_ref, pat_ref, rows_ref, cols_ref, colf_ref, bonds_ref, cracks_ref, d_ref, z_ref, sems = refs[at:]
    n_col = row_ref.shape[0]
    full = 8 * TILE_DEV
    part = 3 * TILE_DEV
    at_row = lax.axis_index("row")
    z, core = at_row // CORES, at_row % CORES
    live = count_ref[0]
    chunks = (live + UNROLL - 1) // UNROLL

    def copies(i):
        part = pl.ds(i * UNROLL, UNROLL)
        return (
            pltpu.make_async_copy(bond_ref.at[part], bonds_ref.at[part], sems.at[0, i]),
            pltpu.make_async_copy(broken_ref.at[part], cracks_ref.at[part], sems.at[1, i]),
        )

    def begin(i, carry):
        for copy in copies(i):
            copy.start()
        return carry

    lax.fori_loop(0, chunks, begin, 0)
    for k, p in enumerate(patterns()):
        pat_ref[k] = p.astype(jnp.bfloat16)
    rowf_ref[...] = jnp.zeros_like(rowf_ref)
    colf_ref[...] = jnp.zeros_like(colf_ref)
    for c in range(n_col):
        rows_ref[c * full:(c + 1) * full] = row_ref[c].reshape(full, TILE)
        if not fresh:
            rows_ref[c * full:c * full + part] = now_row_ref[c].reshape(part, TILE)
    for d in range(n_z):
        src = (z + n_z - d) % n_z
        for j in range(CORES):
            r = src * CORES + (core if j == 0 else 1 - core)
            start = pl.multiple_of(r * full, full)
            cols_ref[pl.ds(start, full)] = col_refs[d][j].reshape(full, TILE)
            if not fresh:
                cols_ref[pl.ds(start, part)] = now_col_refs[d][j].reshape(part, TILE)
    def load(ref, t):
        return ref[pl.ds((t // TILE_DEV) * full + t % TILE_DEV, 8, stride=TILE_DEV), :]

    def add(ref, t, val):
        where = pl.ds((t // TILE_DEV) * part + t % TILE_DEV, 3, stride=TILE_DEV)
        ref[where, :] = ref[where, :] + val[:3]

    own = []
    for j in range(TILE_DEV):
        t = lax.axis_index("col") * TILE_DEV + j
        state = load(rows_ref, t)
        own.append((t, state, features(state, True), features(state, False)))
    ahead = {}
    for j in range(TILE_DEV + LEAD):
        if j < TILE_DEV:
            ahead[j] = lengths(own[j][2][0], own[j][3][0], pat_ref)
        if j >= LEAD:
            t, state, mine, other = own[j - LEAD]
            on_owner = sum_owner(other[1], weights(ahead.pop(j - LEAD), None))
            add(rowf_ref, t, post(on_owner, state, mine[2]))

    def tiles(slot):
        return load(rows_ref, owner_ref[slot]), load(cols_ref, partner_ref[slot])

    def begin_pair(slot):
        alive = jnp.where(slot < live, 1.0, 0.0)
        so, sp = tiles(jnp.minimum(slot, owner_ref.shape[0] - 1))
        fo, fp = features(so, True, alive), features(sp, False, alive)
        return lengths(fo[0], fp[0], pat_ref), fo[1], fp[1]

    def keep(j, begun):
        d_ref[j] = begun[0]
        z_ref[j, 0] = begun[1]
        z_ref[j, 1] = begun[2]

    for j in range(LEAD):
        keep(j, begin_pair(j))

    def body(i, carry):
        for copy in copies(i):
            copy.wait()
        first = i * UNROLL
        begun = {j: (d_ref[j], z_ref[j, 0], z_ref[j, 1]) for j in range(LEAD)}
        sums = []
        for j in range(UNROLL):
            if j + LEAD < UNROLL:
                begun[j + LEAD] = begin_pair(first + j + LEAD)
            d, zo, zp = begun.pop(j)
            w = weights(d, (bonds_ref[first + j], cracks_ref[first + j]))
            sums.append((sum_owner(zp, w), sum_partner(zo, w)))
            if j + LEAD >= UNROLL:
                keep(j + LEAD - UNROLL, begin_pair(first + j + LEAD))
        for j, (on_owner, on_partner) in enumerate(sums):
            so, sp = tiles(first + j)
            alive = jnp.where(first + j < live, 1.0, 0.0)
            add(rowf_ref, owner_ref[first + j], post(on_owner, so, row_of(so, 3) * alive))
            add(colf_ref, partner_ref[first + j], post(on_partner, sp, row_of(sp, 3) * alive))
        return carry

    lax.fori_loop(0, chunks, body, 0)
    for i in range(n_z):
        for ref, c in ((mine_ref, core), (sibling_ref, 1 - core)):
            start = pl.multiple_of((i * CORES + c) * part, part)
            ref[i] = colf_ref[pl.ds(start, part)].reshape(3, TILE_DEV, TILE)


def pair_forces(count, owner, partner, bonds, cracks, row, cols, now_row=None, now_cols=()):
    n_col, n_z = row.shape[0], len(cols)
    fresh = now_row is None
    more = () if fresh else (now_row, *now_cols)
    shares = f32(n_z, 3, TILE_DEV, TILE)
    return pl.pallas_call(
        functools.partial(pair_kernel, n_z, fresh),
        out_shape=(f32(n_col * 3 * TILE_DEV, TILE), shares, shares),
        in_specs=[SMEM] * 3 + [ANY] * 2 + [VMEM] * (1 + n_z + len(more)),
        out_specs=(VMEM,) * 3,
        scratch_shapes=[
            pltpu.VMEM((3, 64, TILE), jnp.bfloat16),
            pltpu.VMEM((n_col * 8 * TILE_DEV, TILE), jnp.float32),
            pltpu.VMEM((n_z * CORES * 8 * TILE_DEV, TILE), jnp.float32),
            pltpu.VMEM((n_z * CORES * 3 * TILE_DEV, TILE), jnp.float32),
            pltpu.VMEM(bonds.shape, bonds.dtype),
            pltpu.VMEM(cracks.shape, cracks.dtype),
            pltpu.VMEM((LEAD, TILE, 3 * TILE), jnp.float32),
            pltpu.VMEM((LEAD, 2, 16, TILE), jnp.bfloat16),
            pltpu.SemaphoreType.DMA((2, bonds.shape[0] // UNROLL)),
        ],
        compiler_params=pltpu.CompilerParams(vmem_limit_bytes=LIMIT),
        name="pair_forces",
    )(count, owner, partner, bonds, cracks, row, *cols, *more)


def start_kernel(moduli_ref, material_ref, rest_ref, disp_ref, vel_ref, acc_ref, spread_ref, state_ref, u_ref, v_ref):
    for c in range(3):
        for t in range(TILE_DEV):
            lanes = pl.ds(t * TILE, TILE)
            v = vel_ref[c:c + 1, lanes] + 0.5 * TIME_STEP * acc_ref[c:c + 1, lanes]
            u = disp_ref[c:c + 1, lanes] + TIME_STEP * v
            x = rest_ref[c:c + 1, lanes] - CENTRE
            v_ref[c, t:t + 1, :] = v
            u_ref[c, t:t + 1, :] = u
            state_ref[c, t:t + 1, :] = x + u
            state_ref[4 + c, t:t + 1, :] = x
    fibre = material_ref[...] == 1
    modulus = jnp.where(fibre, moduli_ref[1], moduli_ref[0])
    state_ref[3] = jnp.sqrt(modulus)
    state_ref[7] = jnp.where(fibre, 1.0, 0.0)
    for i in range(spread_ref.shape[0]):
        spread_ref[i] = state_ref[...]


def start(n_col, moduli, material, rest, disp, vel, acc):
    block = (3, TILE_DEV, TILE)
    return pl.pallas_call(
        start_kernel,
        out_shape=(f32(n_col, 8, TILE_DEV, TILE), f32(8, TILE_DEV, TILE), f32(*block), f32(*block)),
        in_specs=[SMEM] + [VMEM] * 5,
        out_specs=(VMEM,) * 4,
        name="first_half_step",
    )(moduli, material, rest, disp, vel, acc)


def share_kernel(mine_ref, other_ref, *out_refs):
    n_z = len(out_refs)
    z = lax.axis_index("row") // CORES
    for d, out_ref in enumerate(out_refs):
        at = (z + d) % n_z
        out_ref[...] = mine_ref[at] + other_ref[at]


def shares(mine, other):
    n_z = mine.shape[0]
    return pl.pallas_call(
        share_kernel,
        out_shape=(f32(*mine.shape[1:]),) * n_z,
        in_specs=[VMEM] * 2,
        out_specs=(VMEM,) * n_z,
        compiler_params=pltpu.CompilerParams(vmem_limit_bytes=SMALL),
        name="column_shares",
    )(mine, other)


def total(row_ref, col_refs):
    force = row_ref[0]
    for i in range(1, row_ref.shape[0]):
        force = force + row_ref[i]
    for ref in col_refs:
        force = force + ref[...]
    return force


def step_kernel(n_z, row_ref, *refs):
    col_refs = refs[:n_z]
    state_ref, u_ref, v_ref, spread_ref, now_ref, new_u_ref, new_v_ref = refs[n_z:]
    force = total(row_ref, col_refs)
    v = v_ref[...] + TIME_STEP * force
    u = u_ref[...] + TIME_STEP * v
    now = state_ref[4:7] + u
    new_u_ref[...] = u
    new_v_ref[...] = v
    now_ref[...] = now
    for i in range(spread_ref.shape[0]):
        spread_ref[i] = now


def next_step(row, cols, state, u, v):
    return pl.pallas_call(
        functools.partial(step_kernel, len(cols)),
        out_shape=(f32(*row.shape),) + (f32(*u.shape),) * 3,
        in_specs=[VMEM] * (4 + len(cols)),
        out_specs=(VMEM,) * 4,
        compiler_params=pltpu.CompilerParams(vmem_limit_bytes=SMALL),
        name="next_step",
    )(row, *cols, state, u, v)


def last_kernel(n_z, row_ref, *refs):
    col_refs = refs[:n_z]
    u_ref, v_ref, disp_ref, vel_ref = refs[n_z:]
    v = v_ref[...] + 0.5 * TIME_STEP * total(row_ref, col_refs)
    for c in range(3):
        for t in range(TILE_DEV):
            lanes = pl.ds(t * TILE, TILE)
            disp_ref[c:c + 1, lanes] = u_ref[c, t:t + 1, :]
            vel_ref[c:c + 1, lanes] = v[c, t:t + 1, :]


def last_step(row, cols, u, v):
    points = f32(3, TILE_DEV * TILE)
    return pl.pallas_call(
        functools.partial(last_kernel, len(cols)),
        out_shape=(points, points),
        in_specs=[VMEM] * (3 + len(cols)),
        out_specs=(VMEM,) * 2,
        compiler_params=pltpu.CompilerParams(vmem_limit_bytes=SMALL),
        name="last_half_step",
    )(row, *cols, u, v)


def to_sibling(x, n_row):
    return lax.ppermute(x, "row", [(i, i ^ 1) for i in range(n_row)])


def along_z(x, d, n_row):
    n_z = n_row // CORES
    return lax.ppermute(x, "row", [(i, (i // CORES + d) % n_z * CORES + i % CORES) for i in range(n_row)])


def swap(x):
    return lax.all_to_all(x, "col", 0, 0, tiled=True)


def column_gather(block, n_row):
    both = jnp.stack([block, to_sibling(block, n_row)])
    return [both] + [along_z(both, d, n_row) for d in range(1, n_row // CORES)]


def column_sum(mine, sibling, n_row):
    parts = shares(mine, to_sibling(sibling, n_row))
    return [parts[0]] + [along_z(parts[d], d, n_row) for d in range(1, n_row // CORES)]


def per_device(
    rest_pos, displacement, velocity, accel_prev, material, moduli, pair_owner, pair_partner, pair_count, bond_mask, broken
):
    n_row, n_col = lax.axis_size("row"), lax.axis_size("col")
    spread, state, u, v = start(
        n_col, moduli, material.reshape(TILE_DEV, TILE), rest_pos, displacement, velocity, accel_prev
    )
    row = swap(spread)
    cols = column_gather(state, n_row)
    now = ()
    for step in range(STEPS):
        rowf, mine, sibling = pair_forces(pair_count, pair_owner, pair_partner, bond_mask, broken, row, cols, *now)
        row_part = swap(rowf.reshape(n_col, 3, TILE_DEV, TILE))
        col_part = column_sum(mine, sibling, n_row)
        if step < STEPS - 1:
            spread, block, u, v = next_step(row_part, col_part, state, u, v)
            now = (swap(spread), column_gather(block, n_row))
    return last_step(row_part, col_part, u, v)


def solution(mesh):
    points, flat, masks = P(None, ("row", "col")), P(("row", "col")), P(("row", "col"), None, None)
    return jax.shard_map(
        per_device,
        mesh=mesh,
        in_specs=(points,) * 4 + (flat, P()) + (flat,) * 3 + (masks,) * 2,
        out_specs=(points, points),
        check_vma=False,
    )
```

```python
import functools
import math

import jax
import jax.numpy as jnp
from jax import lax
from jax.experimental import pallas as pl
from jax.experimental.pallas import tpu as pltpu
from jax.sharding import PartitionSpec as P

TILE = 128
TILE_DEV = 16
PAIRS_DEV = 128
STEPS = 2
TIME_STEP = 0.5
CENTRE = 2.0
STRENGTH = 1.5 / math.sqrt(TILE * (1.0 + PAIRS_DEV / TILE_DEV))
UNROLL = 16
LEAD = 4
CORES = 2
LIMIT = 50 * 2**20
SMALL = 4 * 2**20
VMEM = pl.BlockSpec(memory_space=pltpu.VMEM)
ANY = pl.BlockSpec(memory_space=pltpu.HBM)
SMEM = pl.BlockSpec(memory_space=pltpu.SMEM)


def f32(*shape):
    return jax.ShapeDtypeStruct(shape, jnp.float32)


def rows_iota(n=8):
    return lax.broadcasted_iota(jnp.int32,(n,TILE),0)

def halves(c):
    c1=c.astype(jnp.bfloat16).astype(jnp.float32)
    return c1,(c-c1).astype(jnp.bfloat16).astype(jnp.float32)

def thirds(c):
    c1,c2=halves(c)
    return c1,c2,(c-c1)-c2

def row_of(s,k):
    return jnp.broadcast_to(s[k:k+1],(8,TILE))

def features(s,owner,alive=None):
    r=rows_iota()
    f=row_of(s,7); m=row_of(s,3)
    if alive is not None:
        m=m*alive
    c1,c2=halves(jnp.where(r==3,f*row_of(s,4),s))
    c=c1+c2
    sq=c*c
    w=jnp.where(r==3,sq,sq+pltpu.roll(sq,7,0)+pltpu.roll(sq,6,0)+0.5)
    z1,z2=halves(m*jnp.where(r==3,1.0,s))
    z=jnp.where(r<4,z1,pltpu.roll(z2,4,0))
    z=jnp.concatenate([z,jnp.zeros_like(z)],0).astype(jnp.bfloat16)
    if owner:
        ones=jnp.where(r==5,f,1.0)
        n=[jnp.where((r==0)|(r==3)|(r==4),t,ones) for t in thirds(w)]
        x=[c1,c1,c2,c2]+n+[jnp.zeros_like(ones)]
    else:
        ones=jnp.where(r==3,f,1.0)
        n=[jnp.where((r==2)|(r==5)|(r==6),t,ones) for t in thirds(pltpu.roll(w,2,0))]
        x=[c1,c2,c1,c2]+n+[jnp.zeros_like(ones)]
    return jnp.concatenate(x,0).astype(jnp.bfloat16),z,m

def patterns():
    row=lax.broadcasted_iota(jnp.int32,(64,TILE),0)
    coord=row<32; spare=row>=56
    row=row%8
    def pick(lo,hi,n1,n2,scale):
        c=jnp.where((row>=lo)&(row<hi),-2.0*scale,0.0)
        n=jnp.where((row==n1)|(row==n2),scale,0.0)
        return jnp.where(spare,0.0,jnp.where(coord,c,n))
    now=pick(0,3,0,2,1.0); rest=pick(4,7,4,6,1.0)
    return now,rest,rest+pick(3,4,3,5,8.0)

def post(acc,s,m):
    t=acc[:8,:TILE]+acc[:8,TILE:]
    t=t+pltpu.roll(t,4,0)
    return (STRENGTH*m)*(t-s*row_of(t,3))

def lengths(left, base, pat_ref, groups=3):
    right = jnp.concatenate([base * pat_ref[k] for k in range(groups)], 1)
    return lax.dot_general(left, right, (((0,), (0,)), ((), ())), preferred_element_type=jnp.float32)


def inverse_lengths(d):
    return lax.rsqrt(jnp.maximum(d[:, :TILE], 1.0)), lax.rsqrt(d[:, TILE:2 * TILE])


def stiffness(d, inv_rest):
    return d[:, 2 * TILE:] * (inv_rest * inv_rest)


def weights(inv_now, inv_rest, stiff):
    w = (inv_rest - inv_now) * stiff
    high = w.astype(jnp.bfloat16)
    return high, (w - high.astype(jnp.float32)).astype(jnp.bfloat16)


def sum_owner(z,w):
    return lax.dot_general(z,jnp.concatenate(w,0),(((1,),(1,)),((),())),preferred_element_type=jnp.float32)

def sum_partner(z,w):
    return jnp.dot(z,jnp.concatenate(w,1),preferred_element_type=jnp.float32)

def pair_kernel(n_row, fresh, ids_ref, *refs):
    if fresh:
        bond_ref, broken_ref, row_ref = refs[:3]
        col_refs = refs[3:2 + n_row]
        rowf_ref, mine_ref, sibling_ref, all_rows_ref, all_cols_ref, all_stiff_ref = refs[2 + n_row:8 + n_row]
        refs = refs[8 + n_row:]
    else:
        all_rows_ref, all_cols_ref, all_stiff_ref, row_ref = refs[:4]
        col_refs = refs[4:3 + n_row]
        rowf_ref, mine_ref, sibling_ref = refs[3 + n_row:6 + n_row]
        refs = refs[6 + n_row:]
    list_ref, pat_ref, rows_ref, cols_ref, colf_ref, stiff_ref, d_ref, z_ref, sems, list_sem, state_sems = refs[:11]
    if fresh:
        bonds_ref, cracks_ref, out_sems = refs[11:]
    n_col, n_z = row_ref.shape[0], n_row // CORES
    full = 8 * TILE_DEV
    part = 3 * TILE_DEV
    at_row = lax.axis_index("row")
    z, core = at_row // CORES, at_row % CORES
    fetch = pltpu.make_async_copy(ids_ref, list_ref, list_sem)
    fetch.start()
    if fresh:
        states = (
            pltpu.make_async_copy(rows_ref, all_rows_ref, state_sems.at[0]),
            pltpu.make_async_copy(cols_ref, all_cols_ref, state_sems.at[1]),
        )
    else:
        states = (
            pltpu.make_async_copy(all_rows_ref, rows_ref, state_sems.at[0]),
            pltpu.make_async_copy(all_cols_ref, cols_ref, state_sems.at[1]),
        )
        for copy in states:
            copy.start()
    for k, p in enumerate(patterns()):
        pat_ref[k] = p.astype(jnp.bfloat16)
    fetch.wait()
    live = list_ref[2, 0].astype(jnp.int32)
    chunks = (live + UNROLL - 1) // UNROLL

    def copies(i):
        part = pl.ds(i * UNROLL, UNROLL)
        if not fresh:
            return (pltpu.make_async_copy(all_stiff_ref.at[part], stiff_ref.at[part], sems.at[0, i]),)
        return (
            pltpu.make_async_copy(bond_ref.at[part], bonds_ref.at[part], sems.at[0, i]),
            pltpu.make_async_copy(broken_ref.at[part], cracks_ref.at[part], sems.at[1, i]),
        )

    def store(i):
        part = pl.ds(i * UNROLL, UNROLL)
        return pltpu.make_async_copy(stiff_ref.at[part], all_stiff_ref.at[part], out_sems.at[i])

    def begin(i, carry):
        for copy in copies(i):
            copy.start()
        return carry

    lax.fori_loop(0, chunks, begin, 0)
    rowf_ref[...] = jnp.zeros_like(rowf_ref)
    colf_ref[...] = jnp.zeros_like(colf_ref)
    if not fresh:
        for copy in states:
            copy.wait()
    roots = (list_ref[3, 0], list_ref[4, 0])

    def place(ref, at, block):
        if not fresh:
            ref[pl.ds(at, part)] = block.reshape(part, TILE)
            return
        ref[pl.ds(at, part)] = block[:3].reshape(part, TILE)
        ref[pl.ds(at + part, TILE_DEV)] = jnp.where(block[6] == 1.0, roots[1], roots[0])
        ref[pl.ds(at + part + TILE_DEV, part + TILE_DEV)] = block[3:].reshape(part + TILE_DEV, TILE)

    for c in range(n_col):
        place(rows_ref, c * full, row_ref[c])
    for d in range(n_z):
        src = (z + n_z - d) % n_z
        for j in range(CORES):
            k = d * CORES + j
            block = row_ref[lax.axis_index("col")] if k == 0 else col_refs[k - 1][...]
            r = src * CORES + (core if j == 0 else 1 - core)
            place(cols_ref, pl.multiple_of(r * full, full), block)
    if fresh:
        for copy in states:
            copy.start()

    def load(ref, t):
        return ref[pl.ds((t // TILE_DEV) * full + t % TILE_DEV, 8, stride=TILE_DEV), :]

    def add(ref, t, val):
        where = pl.ds((t // TILE_DEV) * part + t % TILE_DEV, 3, stride=TILE_DEV)
        ref[where, :] = ref[where, :] + val[:3]

    own = []
    for j in range(TILE_DEV):
        t = lax.axis_index("col") * TILE_DEV + j
        state = load(rows_ref, t)
        own.append((t, state, features(state, True), features(state, False)))
    ahead = {}
    for j in range(TILE_DEV + LEAD):
        if j < TILE_DEV:
            ahead[j] = lengths(own[j][2][0], own[j][3][0], pat_ref)
        if j >= LEAD:
            t, state, mine, other = own[j - LEAD]
            d = ahead.pop(j - LEAD)
            inv_now, inv_rest = inverse_lengths(d)
            on_owner = sum_owner(other[1], weights(inv_now, inv_rest, stiffness(d, inv_rest)))
            add(rowf_ref, t, post(on_owner, state, mine[2]))

    def pair(slot):
        return list_ref[0, slot].astype(jnp.int32), list_ref[1, slot].astype(jnp.int32)

    def tiles(slot):
        o, p = pair(slot)
        return load(rows_ref, o), load(cols_ref, p)

    groups = 3 if fresh else 2

    def begin_pair(slot):
        alive = jnp.where(slot < live, 1.0, 0.0)
        so, sp = tiles(jnp.minimum(slot, PAIRS_DEV - 1))
        fo, fp = features(so, True, alive), features(sp, False, alive)
        return lengths(fo[0], fp[0], pat_ref, groups), fo[1], fp[1]

    def keep(j, begun):
        d_ref[j] = begun[0]
        z_ref[j, 0] = begun[1]
        z_ref[j, 1] = begun[2]

    for j in range(LEAD):
        keep(j, begin_pair(j))

    def body(i, carry):
        for copy in copies(i):
            copy.wait()
        first = i * UNROLL
        begun = {j: (d_ref[j], z_ref[j, 0], z_ref[j, 1]) for j in range(LEAD)}
        sums = []
        for j in range(UNROLL):
            if j + LEAD < UNROLL:
                begun[j + LEAD] = begin_pair(first + j + LEAD)
            d, zo, zp = begun.pop(j)
            inv_now, inv_rest = inverse_lengths(d)
            if fresh:
                stiff = jnp.where(bonds_ref[first + j] > cracks_ref[first + j], stiffness(d, inv_rest), 0.0)
                stiff_ref[first + j] = stiff
            else:
                stiff = stiff_ref[first + j]
            w = weights(inv_now, inv_rest, stiff)
            sums.append((sum_owner(zp, w), sum_partner(zo, w)))
            if j + LEAD >= UNROLL:
                keep(j + LEAD - UNROLL, begin_pair(first + j + LEAD))
        for j, (on_owner, on_partner) in enumerate(sums):
            so, sp = tiles(first + j)
            alive = jnp.where(first + j < live, 1.0, 0.0)
            o, p = pair(first + j)
            add(rowf_ref, o, post(on_owner, so, row_of(so, 3) * alive))
            add(colf_ref, p, post(on_partner, sp, row_of(sp, 3) * alive))
        if fresh:
            store(i).start()
        return carry

    lax.fori_loop(0, chunks, body, 0)
    for i in range(n_z):
        for ref, c in ((mine_ref, core), (sibling_ref, 1 - core)):
            start = pl.multiple_of((i * CORES + c) * part, part)
            ref[i] = colf_ref[pl.ds(start, part)].reshape(3, TILE_DEV, TILE)
    if fresh:
        def finish(i, carry):
            store(i).wait()
            return carry

        lax.fori_loop(0, chunks, finish, 0)
        for copy in states:
            copy.wait()


def pair_forces(ids, row, cols, masks=(), states=()):
    n_col, n_row = row.shape[0], len(cols) + 1
    n_z = n_row // CORES
    fresh = not states
    chunks = PAIRS_DEV // UNROLL
    shares = f32(n_z, 3, TILE_DEV, TILE)
    out = (f32(n_col * 3 * TILE_DEV, TILE), shares, shares)
    held = (f32(n_col * 8 * TILE_DEV, TILE), f32(n_row * 8 * TILE_DEV, TILE), f32(PAIRS_DEV, TILE, TILE))
    inputs = masks if fresh else states
    return pl.pallas_call(
        functools.partial(pair_kernel, n_row, fresh),
        out_shape=out + held if fresh else out,
        in_specs=[ANY] * (1 + len(inputs)) + [VMEM] * n_row,
        out_specs=(VMEM,) * 3 + ((ANY,) * 3 if fresh else ()),
        scratch_shapes=[
            pltpu.SMEM(ids.shape, ids.dtype),
            pltpu.VMEM((3, 64, TILE), jnp.bfloat16),
            pltpu.VMEM(held[0].shape, jnp.float32),
            pltpu.VMEM(held[1].shape, jnp.float32),
            pltpu.VMEM((n_row * 3 * TILE_DEV, TILE), jnp.float32),
            pltpu.VMEM(held[2].shape, jnp.float32),
            pltpu.VMEM((LEAD, TILE, (3 if fresh else 2) * TILE), jnp.float32),
            pltpu.VMEM((LEAD, 2, 16, TILE), jnp.bfloat16),
            pltpu.SemaphoreType.DMA((2, chunks)),
            pltpu.SemaphoreType.DMA,
            pltpu.SemaphoreType.DMA((2,)),
        ] + ([pltpu.VMEM(mask.shape, mask.dtype) for mask in masks] + [pltpu.SemaphoreType.DMA((chunks,))] if fresh else []),
        compiler_params=pltpu.CompilerParams(vmem_limit_bytes=LIMIT),
        name="pair_forces" if fresh else "pair_forces_again",
    )(ids, *inputs, row, *cols)


def start_kernel(
    moduli_ref, count_ref, owner_ref, partner_ref, material_ref, rest_ref, disp_ref, vel_ref, acc_ref,
    spread_ref, state_ref, u_ref, v_ref, ids_ref
):
    ids_ref[0:1] = owner_ref[...].astype(jnp.float32)
    ids_ref[1:2] = partner_ref[...].astype(jnp.float32)
    ids_ref[2:3] = jnp.full((1, TILE), count_ref[0], jnp.int32).astype(jnp.float32)
    for k in range(2):
        ids_ref[3 + k:4 + k] = jnp.sqrt(jnp.full((1, TILE), moduli_ref[k]))
    for c in range(3):
        for t in range(TILE_DEV):
            lanes = pl.ds(t * TILE, TILE)
            v = vel_ref[c:c + 1, lanes] + 0.5 * TIME_STEP * acc_ref[c:c + 1, lanes]
            u = disp_ref[c:c + 1, lanes] + TIME_STEP * v
            x = rest_ref[c:c + 1, lanes] - CENTRE
            v_ref[c, t:t + 1, :] = v
            u_ref[c, t:t + 1, :] = u
            state_ref[c, t:t + 1, :] = x + u
            state_ref[3 + c, t:t + 1, :] = x
    state_ref[6] = material_ref[...].astype(jnp.float32)
    for i in range(spread_ref.shape[0]):
        spread_ref[i] = state_ref[...]


def start(n_col, moduli, count, owner, partner, material, rest, disp, vel, acc):
    block = (3, TILE_DEV, TILE)
    return pl.pallas_call(
        start_kernel,
        out_shape=(f32(n_col, 7, TILE_DEV, TILE), f32(7, TILE_DEV, TILE), f32(*block), f32(*block),
                   f32(5, TILE)),
        in_specs=[SMEM] * 2 + [VMEM] * 7,
        out_specs=(VMEM,) * 5,
        name="first_half_step",
    )(moduli, count, owner, partner, material, rest, disp, vel, acc)


def share_kernel(mine_ref, other_ref, *out_refs):
    n_z = len(out_refs)
    z = lax.axis_index("row") // CORES
    for d, out_ref in enumerate(out_refs):
        at = (z + d) % n_z
        out_ref[...] = mine_ref[at] + other_ref[at]


def shares(mine, other):
    n_z = mine.shape[0]
    return pl.pallas_call(
        share_kernel,
        out_shape=(f32(*mine.shape[1:]),) * n_z,
        in_specs=[VMEM] * 2,
        out_specs=(VMEM,) * n_z,
        compiler_params=pltpu.CompilerParams(vmem_limit_bytes=SMALL),
        name="column_shares",
    )(mine, other)


def total(row_ref, col_refs):
    force = row_ref[0]
    for i in range(1, row_ref.shape[0]):
        force = force + row_ref[i]
    for ref in col_refs:
        force = force + ref[...]
    return force


def step_kernel(n_z, row_ref, *refs):
    col_refs = refs[:n_z]
    state_ref, u_ref, v_ref, spread_ref, now_ref, new_u_ref, new_v_ref = refs[n_z:]
    force = total(row_ref, col_refs)
    v = v_ref[...] + TIME_STEP * force
    u = u_ref[...] + TIME_STEP * v
    now = state_ref[3:6] + u
    new_u_ref[...] = u
    new_v_ref[...] = v
    now_ref[...] = now
    for i in range(spread_ref.shape[0]):
        spread_ref[i] = now


def next_step(row, cols, state, u, v):
    return pl.pallas_call(
        functools.partial(step_kernel, len(cols)),
        out_shape=(f32(*row.shape),) + (f32(*u.shape),) * 3,
        in_specs=[VMEM] * (4 + len(cols)),
        out_specs=(VMEM,) * 4,
        compiler_params=pltpu.CompilerParams(vmem_limit_bytes=SMALL),
        name="next_step",
    )(row, *cols, state, u, v)


def last_kernel(n_z, row_ref, *refs):
    col_refs = refs[:n_z]
    u_ref, v_ref, disp_ref, vel_ref = refs[n_z:]
    v = v_ref[...] + 0.5 * TIME_STEP * total(row_ref, col_refs)
    for c in range(3):
        for t in range(TILE_DEV):
            lanes = pl.ds(t * TILE, TILE)
            disp_ref[c:c + 1, lanes] = u_ref[c, t:t + 1, :]
            vel_ref[c:c + 1, lanes] = v[c, t:t + 1, :]


def last_step(row, cols, u, v):
    points = f32(3, TILE_DEV * TILE)
    return pl.pallas_call(
        functools.partial(last_kernel, len(cols)),
        out_shape=(points, points),
        in_specs=[VMEM] * (3 + len(cols)),
        out_specs=(VMEM,) * 2,
        compiler_params=pltpu.CompilerParams(vmem_limit_bytes=SMALL),
        name="last_half_step",
    )(row, *cols, u, v)


def to_sibling(x, n_row):
    return lax.ppermute(x, "row", [(i, i ^ 1) for i in range(n_row)])


def along_z(x, d, n_row):
    n_z = n_row // CORES
    return lax.ppermute(x, "row", [(i, (i // CORES + d) % n_z * CORES + i % CORES) for i in range(n_row)])


def swap(x):
    return lax.all_to_all(x, "col", 0, 0, tiled=True)


def column_gather(block, n_row):
    blocks = [block] + [along_z(block, d, n_row) for d in range(1, n_row // CORES)]
    return [x for mine in blocks for x in (mine, to_sibling(mine, n_row))][1:]


def column_sum(mine, sibling, n_row):
    parts = shares(mine, to_sibling(sibling, n_row))
    return [parts[0]] + [along_z(parts[d], d, n_row) for d in range(1, n_row // CORES)]


def per_device(
    rest_pos, displacement, velocity, accel_prev, material, moduli, pair_owner, pair_partner, pair_count, bond_mask, broken
):
    n_row, n_col = lax.axis_size("row"), lax.axis_size("col")
    spread, state, u, v, ids = start(
        n_col, moduli, pair_count, pair_owner.reshape(1, -1), pair_partner.reshape(1, -1),
        material.reshape(TILE_DEV, TILE), rest_pos, displacement, velocity, accel_prev
    )
    row, cols, states = swap(spread), column_gather(state, n_row), ()
    for step in range(STEPS):
        rowf, mine, sibling, *held = pair_forces(ids, row, cols, (bond_mask, broken), states)
        row_part = swap(rowf.reshape(n_col, 3, TILE_DEV, TILE))
        col_part = column_sum(mine, sibling, n_row)
        if step < STEPS - 1:
            spread, block, u, v = next_step(row_part, col_part, state, u, v)
            row, cols, states = swap(spread), column_gather(block, n_row), tuple(held)
    return last_step(row_part, col_part, u, v)


def solution(mesh):
    points, flat, masks = P(None, ("row", "col")), P(("row", "col")), P(("row", "col"), None, None)
    return jax.shard_map(
        per_device,
        mesh=mesh,
        in_specs=(points,) * 4 + (flat, P()) + (flat,) * 3 + (masks,) * 2,
        out_specs=(points, points),
        check_vma=False,
    )
```

```python
import functools
import math

import jax
import jax.numpy as jnp
from jax import lax
from jax.experimental import pallas as pl
from jax.experimental.pallas import tpu as pltpu
from jax.sharding import PartitionSpec as P

TILE = 128
TILE_DEV = 16
PAIRS_DEV = 128
STEPS = 2
TIME_STEP = 0.5
CENTRE = 2.0
STRENGTH = 1.5 / math.sqrt(TILE * (1.0 + PAIRS_DEV / TILE_DEV))
UNROLL = 16
LEAD = 5
CORES = 2
LIMIT = 50 * 2**20
SMALL = 4 * 2**20
VMEM = pl.BlockSpec(memory_space=pltpu.VMEM)
ANY = pl.BlockSpec(memory_space=pltpu.HBM)
SMEM = pl.BlockSpec(memory_space=pltpu.SMEM)


def f32(*shape):
    return jax.ShapeDtypeStruct(shape, jnp.float32)


def rows_iota(n=8):
    return lax.broadcasted_iota(jnp.int32,(n,TILE),0)

def halves(c):
    c1=c.astype(jnp.bfloat16).astype(jnp.float32)
    return c1,(c-c1).astype(jnp.bfloat16).astype(jnp.float32)

def thirds(c):
    c1,c2=halves(c)
    return c1,c2,(c-c1)-c2

def row_of(s,k):
    return jnp.broadcast_to(s[k:k+1],(8,TILE))

def features(s,owner,alive=None):
    r=rows_iota()
    f=row_of(s,7); m=row_of(s,3)
    if alive is not None:
        m=m*alive
    c1,c2=halves(jnp.where(r==3,f*row_of(s,4),s))
    c=c1+c2
    sq=c*c
    w=jnp.where(r==3,sq,sq+pltpu.roll(sq,7,0)+pltpu.roll(sq,6,0)+0.5)
    z1,z2=halves(m*jnp.where(r==3,1.0,s))
    z=jnp.where(r<4,z1,pltpu.roll(z2,4,0))
    z=jnp.concatenate([z,jnp.zeros_like(z)],0).astype(jnp.bfloat16)
    if owner:
        ones=jnp.where(r==5,f,1.0)
        n=[jnp.where((r==0)|(r==3)|(r==4),t,ones) for t in thirds(w)]
        x=[c1,c1,c2,c2]+n+[jnp.zeros_like(ones)]
    else:
        ones=jnp.where(r==3,f,1.0)
        n=[jnp.where((r==2)|(r==5)|(r==6),t,ones) for t in thirds(pltpu.roll(w,2,0))]
        x=[c1,c2,c1,c2]+n+[jnp.zeros_like(ones)]
    return jnp.concatenate(x,0).astype(jnp.bfloat16),z,m

def patterns():
    row=lax.broadcasted_iota(jnp.int32,(64,TILE),0)
    coord=row<32; spare=row>=56
    row=row%8
    def pick(lo,hi,n1,n2,scale):
        c=jnp.where((row>=lo)&(row<hi),-2.0*scale,0.0)
        n=jnp.where((row==n1)|(row==n2),scale,0.0)
        return jnp.where(spare,0.0,jnp.where(coord,c,n))
    now=pick(0,3,0,2,1.0); rest=pick(4,7,4,6,1.0)
    return now,rest,rest+pick(3,4,3,5,8.0)

def post(acc,s,m):
    t=acc[:8,:TILE]+acc[:8,TILE:]
    t=t+pltpu.roll(t,4,0)
    return (STRENGTH*m)*(t-s*row_of(t,3))

def lengths(left, base, pat_ref, groups=3):
    right = jnp.concatenate([base * pat_ref[k] for k in range(groups)], 1)
    return lax.dot_general(left, right, (((0,), (0,)), ((), ())), preferred_element_type=jnp.float32)


def inverse_lengths(d):
    return lax.rsqrt(jnp.maximum(d[:, :TILE], 1.0)), lax.rsqrt(d[:, TILE:2 * TILE])


def stiffness(d, inv_rest):
    return d[:, 2 * TILE:] * (inv_rest * inv_rest)


def weights(inv_now, inv_rest, stiff):
    w = (inv_rest - inv_now) * stiff
    high = w.astype(jnp.bfloat16)
    return high, (w - high.astype(jnp.float32)).astype(jnp.bfloat16)


def sum_owner(z,w):
    return lax.dot_general(z,jnp.concatenate(w,0),(((1,),(1,)),((),())),preferred_element_type=jnp.float32)

def sum_partner(z,w):
    return jnp.dot(z,jnp.concatenate(w,1),preferred_element_type=jnp.float32)

def pair_kernel(n_row, fresh, ids_ref, *refs):
    if fresh:
        bond_ref, broken_ref, row_ref = refs[:3]
        col_refs = refs[3:2 + n_row]
        rowf_ref, mine_ref, sibling_ref, all_rows_ref, all_cols_ref, all_stiff_ref = refs[2 + n_row:8 + n_row]
        refs = refs[8 + n_row:]
    else:
        all_rows_ref, all_cols_ref, all_stiff_ref, row_ref = refs[:4]
        col_refs = refs[4:3 + n_row]
        rowf_ref, mine_ref, sibling_ref = refs[3 + n_row:6 + n_row]
        refs = refs[6 + n_row:]
    list_ref, pat_ref, rows_ref, cols_ref, colf_ref, stiff_ref, d_ref, z_ref, sems, list_sem, state_sems = refs[:11]
    if fresh:
        bonds_ref, cracks_ref, out_sems = refs[11:]
    n_col, n_z = row_ref.shape[0], n_row // CORES
    full = 8 * TILE_DEV
    part = 3 * TILE_DEV
    at_row = lax.axis_index("row")
    z, core = at_row // CORES, at_row % CORES
    fetch = pltpu.make_async_copy(ids_ref, list_ref, list_sem)
    fetch.start()

    def copies(i):
        part = pl.ds(i * UNROLL, UNROLL)
        if not fresh:
            return (pltpu.make_async_copy(all_stiff_ref.at[part], stiff_ref.at[part], sems.at[0, i]),)
        return (
            pltpu.make_async_copy(bond_ref.at[part], bonds_ref.at[part], sems.at[0, i]),
            pltpu.make_async_copy(broken_ref.at[part], cracks_ref.at[part], sems.at[1, i]),
        )

    def store(i):
        part = pl.ds(i * UNROLL, UNROLL)
        return pltpu.make_async_copy(stiff_ref.at[part], all_stiff_ref.at[part], out_sems.at[i])

    def begin(i, carry):
        for copy in copies(i):
            copy.start()
        return carry

    begin(0, 0)
    if fresh:
        states = (
            pltpu.make_async_copy(rows_ref, all_rows_ref, state_sems.at[0]),
            pltpu.make_async_copy(cols_ref, all_cols_ref, state_sems.at[1]),
        )
    else:
        states = (
            pltpu.make_async_copy(all_rows_ref, rows_ref, state_sems.at[0]),
            pltpu.make_async_copy(all_cols_ref, cols_ref, state_sems.at[1]),
        )
        for copy in states:
            copy.start()
    for k, p in enumerate(patterns()):
        pat_ref[k] = p.astype(jnp.bfloat16)
    fetch.wait()
    live = list_ref[2, 0].astype(jnp.int32)
    chunks = (live + UNROLL - 1) // UNROLL

    lax.fori_loop(1, chunks, begin, 0)
    rowf_ref[...] = jnp.zeros_like(rowf_ref)
    colf_ref[...] = jnp.zeros_like(colf_ref)
    if not fresh:
        for copy in states:
            copy.wait()
    roots = (list_ref[3, 0], list_ref[4, 0])

    def place(ref, at, block):
        if not fresh:
            ref[pl.ds(at, part)] = block.reshape(part, TILE)
            return
        ref[pl.ds(at, part)] = block[:3].reshape(part, TILE)
        ref[pl.ds(at + part, TILE_DEV)] = jnp.where(block[6] == 1.0, roots[1], roots[0])
        ref[pl.ds(at + part + TILE_DEV, part + TILE_DEV)] = block[3:].reshape(part + TILE_DEV, TILE)

    for c in range(n_col):
        place(rows_ref, c * full, row_ref[c])
    for d in range(n_z):
        src = (z + n_z - d) % n_z
        for j in range(CORES):
            k = d * CORES + j
            block = row_ref[lax.axis_index("col")] if k == 0 else col_refs[k - 1][...]
            r = src * CORES + (core if j == 0 else 1 - core)
            place(cols_ref, pl.multiple_of(r * full, full), block)
    if fresh:
        for copy in states:
            copy.start()

    def load(ref, t):
        return ref[pl.ds((t // TILE_DEV) * full + t % TILE_DEV, 8, stride=TILE_DEV), :]

    def add(ref, t, val):
        where = pl.ds((t // TILE_DEV) * part + t % TILE_DEV, 3, stride=TILE_DEV)
        ref[where, :] = ref[where, :] + val[:3]

    own = []
    for j in range(TILE_DEV):
        t = lax.axis_index("col") * TILE_DEV + j
        state = load(rows_ref, t)
        own.append((t, state, features(state, True), features(state, False)))
    ahead = {}
    for j in range(TILE_DEV + LEAD):
        if j < TILE_DEV:
            ahead[j] = lengths(own[j][2][0], own[j][3][0], pat_ref)
        if j >= LEAD:
            t, state, mine, other = own[j - LEAD]
            d = ahead.pop(j - LEAD)
            inv_now, inv_rest = inverse_lengths(d)
            on_owner = sum_owner(other[1], weights(inv_now, inv_rest, stiffness(d, inv_rest)))
            add(rowf_ref, t, post(on_owner, state, mine[2]))

    def pair(slot):
        return list_ref[0, slot].astype(jnp.int32), list_ref[1, slot].astype(jnp.int32)

    def tiles(slot):
        o, p = pair(slot)
        return load(rows_ref, o), load(cols_ref, p)

    groups = 3 if fresh else 2

    def begin_pair(slot):
        alive = jnp.where(slot < live, 1.0, 0.0)
        so, sp = tiles(jnp.minimum(slot, PAIRS_DEV - 1))
        fo, fp = features(so, True, alive), features(sp, False, alive)
        return lengths(fo[0], fp[0], pat_ref, groups), fo[1], fp[1]

    def keep(j, begun):
        d_ref[j] = begun[0]
        z_ref[j, 0] = begun[1]
        z_ref[j, 1] = begun[2]

    for j in range(LEAD):
        keep(j, begin_pair(j))

    def body(i, carry):
        for copy in copies(i):
            copy.wait()
        first = i * UNROLL
        begun = {j: (d_ref[j], z_ref[j, 0], z_ref[j, 1]) for j in range(LEAD)}
        sums = []
        for j in range(UNROLL):
            if j + LEAD < UNROLL:
                begun[j + LEAD] = begin_pair(first + j + LEAD)
            d, zo, zp = begun.pop(j)
            inv_now, inv_rest = inverse_lengths(d)
            if fresh:
                stiff = jnp.where(bonds_ref[first + j] > cracks_ref[first + j], stiffness(d, inv_rest), 0.0)
                stiff_ref[first + j] = stiff
            else:
                stiff = stiff_ref[first + j]
            w = weights(inv_now, inv_rest, stiff)
            sums.append((sum_owner(zp, w), sum_partner(zo, w)))
            if j + LEAD >= UNROLL:
                keep(j + LEAD - UNROLL, begin_pair(first + j + LEAD))
        for j, (on_owner, on_partner) in enumerate(sums):
            so, sp = tiles(first + j)
            alive = jnp.where(first + j < live, 1.0, 0.0)
            o, p = pair(first + j)
            add(rowf_ref, o, post(on_owner, so, row_of(so, 3) * alive))
            add(colf_ref, p, post(on_partner, sp, row_of(sp, 3) * alive))
        if fresh:
            store(i).start()
        return carry

    lax.fori_loop(0, chunks, body, 0)
    for i in range(n_z):
        for ref, c in ((mine_ref, core), (sibling_ref, 1 - core)):
            start = pl.multiple_of((i * CORES + c) * part, part)
            ref[i] = colf_ref[pl.ds(start, part)].reshape(3, TILE_DEV, TILE)
    if fresh:
        def finish(i, carry):
            store(i).wait()
            return carry

        lax.fori_loop(0, chunks, finish, 0)
        for copy in states:
            copy.wait()


def pair_forces(ids, row, cols, masks=(), states=()):
    n_col, n_row = row.shape[0], len(cols) + 1
    n_z = n_row // CORES
    fresh = not states
    chunks = PAIRS_DEV // UNROLL
    shares = f32(n_z, 3, TILE_DEV, TILE)
    out = (f32(n_col * 3 * TILE_DEV, TILE), shares, shares)
    held = (f32(n_col * 8 * TILE_DEV, TILE), f32(n_row * 8 * TILE_DEV, TILE), f32(PAIRS_DEV, TILE, TILE))
    inputs = masks if fresh else states
    return pl.pallas_call(
        functools.partial(pair_kernel, n_row, fresh),
        out_shape=out + held if fresh else out,
        in_specs=[ANY] * (1 + len(inputs)) + [VMEM] * n_row,
        out_specs=(VMEM,) * 3 + ((ANY,) * 3 if fresh else ()),
        scratch_shapes=[
            pltpu.SMEM(ids.shape, ids.dtype),
            pltpu.VMEM((3, 64, TILE), jnp.bfloat16),
            pltpu.VMEM(held[0].shape, jnp.float32),
            pltpu.VMEM(held[1].shape, jnp.float32),
            pltpu.VMEM((n_row * 3 * TILE_DEV, TILE), jnp.float32),
            pltpu.VMEM(held[2].shape, jnp.float32),
            pltpu.VMEM((LEAD, TILE, (3 if fresh else 2) * TILE), jnp.float32),
            pltpu.VMEM((LEAD, 2, 16, TILE), jnp.bfloat16),
            pltpu.SemaphoreType.DMA((2, chunks)),
            pltpu.SemaphoreType.DMA,
            pltpu.SemaphoreType.DMA((2,)),
        ] + ([pltpu.VMEM(mask.shape, mask.dtype) for mask in masks] + [pltpu.SemaphoreType.DMA((chunks,))] if fresh else []),
        compiler_params=pltpu.CompilerParams(vmem_limit_bytes=LIMIT),
        name="pair_forces" if fresh else "pair_forces_again",
    )(ids, *inputs, row, *cols)


def start_kernel(
    moduli_ref, count_ref, owner_ref, partner_ref, material_ref, rest_ref, disp_ref, vel_ref, acc_ref,
    spread_ref, state_ref, u_ref, v_ref, ids_ref
):
    ids_ref[0:1] = owner_ref[...].astype(jnp.float32)
    ids_ref[1:2] = partner_ref[...].astype(jnp.float32)
    ids_ref[2:3] = jnp.full((1, TILE), count_ref[0], jnp.int32).astype(jnp.float32)
    for k in range(2):
        ids_ref[3 + k:4 + k] = jnp.sqrt(jnp.full((1, TILE), moduli_ref[k]))
    for c in range(3):
        for t in range(TILE_DEV):
            lanes = pl.ds(t * TILE, TILE)
            v = vel_ref[c:c + 1, lanes] + 0.5 * TIME_STEP * acc_ref[c:c + 1, lanes]
            u = disp_ref[c:c + 1, lanes] + TIME_STEP * v
            x = rest_ref[c:c + 1, lanes] - CENTRE
            v_ref[c, t:t + 1, :] = v
            u_ref[c, t:t + 1, :] = u
            state_ref[c, t:t + 1, :] = x + u
            state_ref[3 + c, t:t + 1, :] = x
    state_ref[6] = material_ref[...].astype(jnp.float32)
    for i in range(spread_ref.shape[0]):
        spread_ref[i] = state_ref[...]


def start(n_col, moduli, count, owner, partner, material, rest, disp, vel, acc):
    block = (3, TILE_DEV, TILE)
    return pl.pallas_call(
        start_kernel,
        out_shape=(f32(n_col, 7, TILE_DEV, TILE), f32(7, TILE_DEV, TILE), f32(*block), f32(*block),
                   f32(5, TILE)),
        in_specs=[SMEM] * 2 + [VMEM] * 7,
        out_specs=(VMEM,) * 5,
        name="first_half_step",
    )(moduli, count, owner, partner, material, rest, disp, vel, acc)


def share_kernel(mine_ref, other_ref, *out_refs):
    n_z = len(out_refs)
    z = lax.axis_index("row") // CORES
    for d, out_ref in enumerate(out_refs):
        at = (z + d) % n_z
        out_ref[...] = mine_ref[at] + other_ref[at]


def shares(mine, other):
    n_z = mine.shape[0]
    return pl.pallas_call(
        share_kernel,
        out_shape=(f32(*mine.shape[1:]),) * n_z,
        in_specs=[VMEM] * 2,
        out_specs=(VMEM,) * n_z,
        compiler_params=pltpu.CompilerParams(vmem_limit_bytes=SMALL),
        name="column_shares",
    )(mine, other)


def total(row_ref, col_refs):
    force = row_ref[0]
    for i in range(1, row_ref.shape[0]):
        force = force + row_ref[i]
    for ref in col_refs:
        force = force + ref[...]
    return force


def step_kernel(n_z, row_ref, *refs):
    col_refs = refs[:n_z]
    state_ref, u_ref, v_ref, spread_ref, now_ref, new_u_ref, new_v_ref = refs[n_z:]
    force = total(row_ref, col_refs)
    v = v_ref[...] + TIME_STEP * force
    u = u_ref[...] + TIME_STEP * v
    now = state_ref[3:6] + u
    new_u_ref[...] = u
    new_v_ref[...] = v
    now_ref[...] = now
    for i in range(spread_ref.shape[0]):
        spread_ref[i] = now


def next_step(row, cols, state, u, v):
    return pl.pallas_call(
        functools.partial(step_kernel, len(cols)),
        out_shape=(f32(*row.shape),) + (f32(*u.shape),) * 3,
        in_specs=[VMEM] * (4 + len(cols)),
        out_specs=(VMEM,) * 4,
        compiler_params=pltpu.CompilerParams(vmem_limit_bytes=SMALL),
        name="next_step",
    )(row, *cols, state, u, v)


def last_kernel(n_z, row_ref, *refs):
    col_refs = refs[:n_z]
    u_ref, v_ref, disp_ref, vel_ref = refs[n_z:]
    v = v_ref[...] + 0.5 * TIME_STEP * total(row_ref, col_refs)
    for c in range(3):
        for t in range(TILE_DEV):
            lanes = pl.ds(t * TILE, TILE)
            disp_ref[c:c + 1, lanes] = u_ref[c, t:t + 1, :]
            vel_ref[c:c + 1, lanes] = v[c, t:t + 1, :]


def last_step(row, cols, u, v):
    points = f32(3, TILE_DEV * TILE)
    return pl.pallas_call(
        functools.partial(last_kernel, len(cols)),
        out_shape=(points, points),
        in_specs=[VMEM] * (3 + len(cols)),
        out_specs=(VMEM,) * 2,
        compiler_params=pltpu.CompilerParams(vmem_limit_bytes=SMALL),
        name="last_half_step",
    )(row, *cols, u, v)


def to_sibling(x, n_row):
    return lax.ppermute(x, "row", [(i, i ^ 1) for i in range(n_row)])


def along_z(x, d, n_row):
    n_z = n_row // CORES
    return lax.ppermute(x, "row", [(i, (i // CORES + d) % n_z * CORES + i % CORES) for i in range(n_row)])


def swap(x):
    return lax.all_to_all(x, "col", 0, 0, tiled=True)


def column_gather(block, n_row):
    blocks = [block] + [along_z(block, d, n_row) for d in range(1, n_row // CORES)]
    return [x for mine in blocks for x in (mine, to_sibling(mine, n_row))][1:]


def column_sum(mine, sibling, n_row):
    parts = shares(mine, to_sibling(sibling, n_row))
    return [parts[0]] + [along_z(parts[d], d, n_row) for d in range(1, n_row // CORES)]


def per_device(
    rest_pos, displacement, velocity, accel_prev, material, moduli, pair_owner, pair_partner, pair_count, bond_mask, broken
):
    n_row, n_col = lax.axis_size("row"), lax.axis_size("col")
    spread, state, u, v, ids = start(
        n_col, moduli, pair_count, pair_owner.reshape(1, -1), pair_partner.reshape(1, -1),
        material.reshape(TILE_DEV, TILE), rest_pos, displacement, velocity, accel_prev
    )
    row, cols, states = swap(spread), column_gather(state, n_row), ()
    for step in range(STEPS):
        rowf, mine, sibling, *held = pair_forces(ids, row, cols, (bond_mask, broken), states)
        row_part = swap(rowf.reshape(n_col, 3, TILE_DEV, TILE))
        col_part = column_sum(mine, sibling, n_row)
        if step < STEPS - 1:
            spread, block, u, v = next_step(row_part, col_part, state, u, v)
            row, cols, states = swap(spread), column_gather(block, n_row), tuple(held)
    return last_step(row_part, col_part, u, v)


def solution(mesh):
    points, flat, masks = P(None, ("row", "col")), P(("row", "col")), P(("row", "col"), None, None)
    return jax.shard_map(
        per_device,
        mesh=mesh,
        in_specs=(points,) * 4 + (flat, P()) + (flat,) * 3 + (masks,) * 2,
        out_specs=(points, points),
        check_vma=False,
    )
```

```python
import functools
import math

import jax
import jax.numpy as jnp
from jax import lax
from jax.experimental import pallas as pl
from jax.experimental.pallas import tpu as pltpu
from jax.sharding import PartitionSpec as P

TILE = 128
TILE_DEV = 16
PAIRS_DEV = 128
STEPS = 2
TIME_STEP = 0.5
CENTRE = 2.0
STRENGTH = 1.5 / math.sqrt(TILE * (1.0 + PAIRS_DEV / TILE_DEV))
UNROLL = 16
LEAD = 5
CORES = 2
LIMIT = 50 * 2**20
SMALL = 4 * 2**20
VMEM = pl.BlockSpec(memory_space=pltpu.VMEM)
ANY = pl.BlockSpec(memory_space=pltpu.HBM)
SMEM = pl.BlockSpec(memory_space=pltpu.SMEM)


def f32(*shape):
    return jax.ShapeDtypeStruct(shape, jnp.float32)


def rows_iota(n=8):
    return lax.broadcasted_iota(jnp.int32,(n,TILE),0)

def halves(c):
    c1=c.astype(jnp.bfloat16).astype(jnp.float32)
    return c1,(c-c1).astype(jnp.bfloat16).astype(jnp.float32)

def thirds(c):
    c1,c2=halves(c)
    return c1,c2,(c-c1)-c2

def row_of(s,k):
    return jnp.broadcast_to(s[k:k+1],(8,TILE))

def features(s,owner,alive=None):
    r=rows_iota()
    f=row_of(s,7); m=row_of(s,3)
    if alive is not None:
        m=m*alive
    c1,c2=halves(jnp.where(r==3,f*row_of(s,4),s))
    c=c1+c2
    sq=c*c
    w=jnp.where(r==3,sq,sq+pltpu.roll(sq,7,0)+pltpu.roll(sq,6,0)+0.5)
    z1,z2=halves(m*jnp.where(r==3,1.0,s))
    z=jnp.where(r<4,z1,pltpu.roll(z2,4,0))
    z=jnp.concatenate([z,jnp.zeros_like(z)],0).astype(jnp.bfloat16)
    if owner:
        ones=jnp.where(r==5,f,1.0)
        n=[jnp.where((r==0)|(r==3)|(r==4),t,ones) for t in thirds(w)]
        x=[c1,c1,c2,c2]+n+[jnp.zeros_like(ones)]
    else:
        ones=jnp.where(r==3,f,1.0)
        n=[jnp.where((r==2)|(r==5)|(r==6),t,ones) for t in thirds(pltpu.roll(w,2,0))]
        x=[c1,c2,c1,c2]+n+[jnp.zeros_like(ones)]
    return jnp.concatenate(x,0).astype(jnp.bfloat16),z,m

def patterns():
    row=lax.broadcasted_iota(jnp.int32,(64,TILE),0)
    coord=row<32; spare=row>=56
    row=row%8
    def pick(lo,hi,n1,n2,scale):
        c=jnp.where((row>=lo)&(row<hi),-2.0*scale,0.0)
        n=jnp.where((row==n1)|(row==n2),scale,0.0)
        return jnp.where(spare,0.0,jnp.where(coord,c,n))
    now=pick(0,3,0,2,1.0); rest=pick(4,7,4,6,1.0)
    return now,rest,rest+pick(3,4,3,5,8.0)

def post(acc,s,m):
    t=acc[:8,:TILE]+acc[:8,TILE:]
    t=t+pltpu.roll(t,4,0)
    return (STRENGTH*m)*(t-s*row_of(t,3))

def lengths(left, base, pat_ref, groups=3):
    right = jnp.concatenate([base * pat_ref[k] for k in range(groups)], 1)
    return lax.dot_general(left, right, (((0,), (0,)), ((), ())), preferred_element_type=jnp.float32)


def inverse_lengths(d):
    return lax.rsqrt(jnp.maximum(d[:, :TILE], 1.0)), lax.rsqrt(d[:, TILE:2 * TILE])


def stiffness(d, inv_rest):
    return d[:, 2 * TILE:] * (inv_rest * inv_rest)


def weights(inv_now, inv_rest, stiff):
    w = (inv_rest - inv_now) * stiff
    high = w.astype(jnp.bfloat16)
    return high, (w - high.astype(jnp.float32)).astype(jnp.bfloat16)


def sum_owner(z,w):
    return lax.dot_general(z,jnp.concatenate(w,0),(((1,),(1,)),((),())),preferred_element_type=jnp.float32)

def sum_partner(z,w):
    return jnp.dot(z,jnp.concatenate(w,1),preferred_element_type=jnp.float32)

def pair_kernel(n_row, fresh, ids_ref, *refs):
    if fresh:
        bond_ref, broken_ref, row_ref = refs[:3]
        col_refs = refs[3:2 + n_row]
        rowf_ref, mine_ref, sibling_ref, all_rows_ref, all_cols_ref, all_stiff_ref = refs[2 + n_row:8 + n_row]
        refs = refs[8 + n_row:]
    else:
        all_rows_ref, all_cols_ref, all_stiff_ref, row_ref = refs[:4]
        col_refs = refs[4:3 + n_row]
        rowf_ref, mine_ref, sibling_ref = refs[3 + n_row:6 + n_row]
        refs = refs[6 + n_row:]
    list_ref, pat_ref, rows_ref, cols_ref, colf_ref, rowsum_ref, stiff_ref, d_ref, z_ref, sems, list_sem, state_sems = refs[:12]
    if fresh:
        bonds_ref, cracks_ref, out_sems = refs[12:]
    n_col, n_z = row_ref.shape[0], n_row // CORES
    full = 8 * TILE_DEV
    part = 3 * TILE_DEV
    at_row = lax.axis_index("row")
    z, core = at_row // CORES, at_row % CORES
    fetch = pltpu.make_async_copy(ids_ref, list_ref, list_sem)
    fetch.start()

    def copies(i):
        part = pl.ds(i * UNROLL, UNROLL)
        if not fresh:
            return (pltpu.make_async_copy(all_stiff_ref.at[part], stiff_ref.at[part], sems.at[0, i]),)
        return (
            pltpu.make_async_copy(bond_ref.at[part], bonds_ref.at[part], sems.at[0, i]),
            pltpu.make_async_copy(broken_ref.at[part], cracks_ref.at[part], sems.at[1, i]),
        )

    def store(i):
        part = pl.ds(i * UNROLL, UNROLL)
        return pltpu.make_async_copy(stiff_ref.at[part], all_stiff_ref.at[part], out_sems.at[i])

    def begin(i, carry):
        for copy in copies(i):
            copy.start()
        return carry

    begin(0, 0)
    used_rows = rows_ref.at[pl.ds(0, n_col * full)]
    used_cols = cols_ref.at[pl.ds(0, n_row * full)]
    if fresh:
        states = (
            pltpu.make_async_copy(used_rows, all_rows_ref, state_sems.at[0]),
            pltpu.make_async_copy(used_cols, all_cols_ref, state_sems.at[1]),
        )
    else:
        states = (
            pltpu.make_async_copy(all_rows_ref, used_rows, state_sems.at[0]),
            pltpu.make_async_copy(all_cols_ref, used_cols, state_sems.at[1]),
        )
        for copy in states:
            copy.start()
    for k, p in enumerate(patterns()):
        pat_ref[k] = p.astype(jnp.bfloat16)
    fetch.wait()
    live = list_ref[2, 0].astype(jnp.int32)
    chunks = (live + UNROLL - 1) // UNROLL

    lax.fori_loop(1, chunks, begin, 0)
    rowsum_ref[...] = jnp.zeros_like(rowsum_ref)
    colf_ref[...] = jnp.zeros_like(colf_ref)
    if not fresh:
        for copy in states:
            copy.wait()
    roots = (list_ref[3, 0], list_ref[4, 0])

    def place(ref, at, block):
        if not fresh:
            ref[pl.ds(at, part)] = block.reshape(part, TILE)
            return
        ref[pl.ds(at, part)] = block[:3].reshape(part, TILE)
        ref[pl.ds(at + part, TILE_DEV)] = jnp.where(block[6] == 1.0, roots[1], roots[0])
        ref[pl.ds(at + part + TILE_DEV, part + TILE_DEV)] = block[3:].reshape(part + TILE_DEV, TILE)

    for c in range(n_col):
        place(rows_ref, c * full, row_ref[c])
    for d in range(n_z):
        src = (z + n_z - d) % n_z
        for j in range(CORES):
            k = d * CORES + j
            block = row_ref[lax.axis_index("col")] if k == 0 else col_refs[k - 1][...]
            r = src * CORES + (core if j == 0 else 1 - core)
            place(cols_ref, pl.multiple_of(r * full, full), block)
    if fresh:
        for copy in states:
            copy.start()

    def load(ref, t):
        return ref[pl.ds((t // TILE_DEV) * full + t % TILE_DEV, 8, stride=TILE_DEV), :]

    def add(ref, t, val):
        where = pl.ds((t // TILE_DEV) * part + t % TILE_DEV, 3, stride=TILE_DEV)
        ref[where, :] = ref[where, :] + val[:3]

    own = []
    for j in range(TILE_DEV):
        t = lax.axis_index("col") * TILE_DEV + j
        state = load(rows_ref, t)
        own.append((t, state, features(state, True), features(state, False)))
    ahead = {}
    for j in range(TILE_DEV + LEAD):
        if j < TILE_DEV:
            ahead[j] = lengths(own[j][2][0], own[j][3][0], pat_ref)
        if j >= LEAD:
            t, state, mine, other = own[j - LEAD]
            d = ahead.pop(j - LEAD)
            inv_now, inv_rest = inverse_lengths(d)
            on_owner = sum_owner(other[1], weights(inv_now, inv_rest, stiffness(d, inv_rest)))
            add(rowsum_ref, t, post(on_owner, state, mine[2]))

    def pair(slot):
        return list_ref[0, slot].astype(jnp.int32), list_ref[1, slot].astype(jnp.int32)

    def tiles(slot):
        o, p = pair(slot)
        return load(rows_ref, o), load(cols_ref, p)

    groups = 3 if fresh else 2

    def begin_pair(slot):
        alive = jnp.where(slot < live, 1.0, 0.0)
        so, sp = tiles(jnp.minimum(slot, PAIRS_DEV - 1))
        fo, fp = features(so, True, alive), features(sp, False, alive)
        return lengths(fo[0], fp[0], pat_ref, groups), fo[1], fp[1]

    def keep(j, begun):
        d_ref[j] = begun[0]
        z_ref[j, 0] = begun[1]
        z_ref[j, 1] = begun[2]

    for j in range(LEAD):
        keep(j, begin_pair(j))

    def body(i, carry):
        for copy in copies(i):
            copy.wait()
        first = i * UNROLL
        begun = {j: (d_ref[j], z_ref[j, 0], z_ref[j, 1]) for j in range(LEAD)}
        sums = []
        for j in range(UNROLL):
            if j + LEAD < UNROLL:
                begun[j + LEAD] = begin_pair(first + j + LEAD)
            d, zo, zp = begun.pop(j)
            inv_now, inv_rest = inverse_lengths(d)
            if fresh:
                stiff = jnp.where(bonds_ref[first + j] > cracks_ref[first + j], stiffness(d, inv_rest), 0.0)
                stiff_ref[first + j] = stiff
            else:
                stiff = stiff_ref[first + j]
            w = weights(inv_now, inv_rest, stiff)
            sums.append((sum_owner(zp, w), sum_partner(zo, w)))
            if j + LEAD >= UNROLL:
                keep(j + LEAD - UNROLL, begin_pair(first + j + LEAD))
        for j, (on_owner, on_partner) in enumerate(sums):
            so, sp = tiles(first + j)
            alive = jnp.where(first + j < live, 1.0, 0.0)
            o, p = pair(first + j)
            add(rowsum_ref, o, post(on_owner, so, row_of(so, 3) * alive))
            add(colf_ref, p, post(on_partner, sp, row_of(sp, 3) * alive))
        if fresh:
            store(i).start()
        return carry

    lax.fori_loop(0, chunks, body, 0)
    rowf_ref[...] = rowsum_ref[:n_col * part]
    for i in range(n_z):
        for ref, c in ((mine_ref, core), (sibling_ref, 1 - core)):
            start = pl.multiple_of((i * CORES + c) * part, part)
            ref[i] = colf_ref[pl.ds(start, part)].reshape(3, TILE_DEV, TILE)
    if fresh:
        def finish(i, carry):
            store(i).wait()
            return carry

        lax.fori_loop(0, chunks, finish, 0)
        for copy in states:
            copy.wait()


def pair_forces(ids, row, cols, masks=(), states=()):
    n_col, n_row = row.shape[0], len(cols) + 1
    n_z = n_row // CORES
    fresh = not states
    chunks = PAIRS_DEV // UNROLL
    shares = f32(n_z, 3, TILE_DEV, TILE)
    out = (f32(n_col * 3 * TILE_DEV, TILE), shares, shares)
    held = (f32(n_col * 8 * TILE_DEV, TILE), f32(n_row * 8 * TILE_DEV, TILE), f32(PAIRS_DEV, TILE, TILE))
    inputs = masks if fresh else states
    return pl.pallas_call(
        functools.partial(pair_kernel, n_row, fresh),
        out_shape=out + held if fresh else out,
        in_specs=[ANY] * (1 + len(inputs)) + [VMEM] * n_row,
        out_specs=(VMEM,) * 3 + ((ANY,) * 3 if fresh else ()),
        scratch_shapes=[
            pltpu.SMEM(ids.shape, ids.dtype),
            pltpu.VMEM((3, 64, TILE), jnp.bfloat16),
            pltpu.VMEM((held[0].shape[0] + 8 * TILE_DEV, TILE), jnp.float32),
            pltpu.VMEM((held[1].shape[0] + 8 * TILE_DEV, TILE), jnp.float32),
            pltpu.VMEM(((n_row + 1) * 3 * TILE_DEV, TILE), jnp.float32),
            pltpu.VMEM(((n_col + 1) * 3 * TILE_DEV, TILE), jnp.float32),
            pltpu.VMEM(held[2].shape, jnp.float32),
            pltpu.VMEM((LEAD, TILE, (3 if fresh else 2) * TILE), jnp.float32),
            pltpu.VMEM((LEAD, 2, 16, TILE), jnp.bfloat16),
            pltpu.SemaphoreType.DMA((2, chunks)),
            pltpu.SemaphoreType.DMA,
            pltpu.SemaphoreType.DMA((2,)),
        ] + ([pltpu.VMEM(mask.shape, mask.dtype) for mask in masks] + [pltpu.SemaphoreType.DMA((chunks,))] if fresh else []),
        compiler_params=pltpu.CompilerParams(vmem_limit_bytes=LIMIT),
        name="pair_forces" if fresh else "pair_forces_again",
    )(ids, *inputs, row, *cols)


def start_kernel(
    moduli_ref, count_ref, owner_ref, partner_ref, material_ref, rest_ref, disp_ref, vel_ref, acc_ref,
    spread_ref, state_ref, u_ref, v_ref, ids_ref
):
    ids_ref[0:1] = owner_ref[...].astype(jnp.float32)
    ids_ref[1:2] = partner_ref[...].astype(jnp.float32)
    ids_ref[2:3] = jnp.full((1, TILE), count_ref[0], jnp.int32).astype(jnp.float32)
    for k in range(2):
        ids_ref[3 + k:4 + k] = jnp.sqrt(jnp.full((1, TILE), moduli_ref[k]))
    for c in range(3):
        for t in range(TILE_DEV):
            lanes = pl.ds(t * TILE, TILE)
            v = vel_ref[c:c + 1, lanes] + 0.5 * TIME_STEP * acc_ref[c:c + 1, lanes]
            u = disp_ref[c:c + 1, lanes] + TIME_STEP * v
            x = rest_ref[c:c + 1, lanes] - CENTRE
            v_ref[c, t:t + 1, :] = v
            u_ref[c, t:t + 1, :] = u
            state_ref[c, t:t + 1, :] = x + u
            state_ref[3 + c, t:t + 1, :] = x
    state_ref[6] = material_ref[...].astype(jnp.float32)
    for i in range(spread_ref.shape[0]):
        spread_ref[i] = state_ref[...]


def start(n_col, moduli, count, owner, partner, material, rest, disp, vel, acc):
    block = (3, TILE_DEV, TILE)
    return pl.pallas_call(
        start_kernel,
        out_shape=(f32(n_col, 7, TILE_DEV, TILE), f32(7, TILE_DEV, TILE), f32(*block), f32(*block),
                   f32(5, TILE)),
        in_specs=[SMEM] * 2 + [VMEM] * 7,
        out_specs=(VMEM,) * 5,
        name="first_half_step",
    )(moduli, count, owner, partner, material, rest, disp, vel, acc)


def share_kernel(mine_ref, other_ref, *out_refs):
    n_z = len(out_refs)
    z = lax.axis_index("row") // CORES
    for d, out_ref in enumerate(out_refs):
        at = (z + d) % n_z
        out_ref[...] = mine_ref[at] + other_ref[at]


def shares(mine, other):
    n_z = mine.shape[0]
    return pl.pallas_call(
        share_kernel,
        out_shape=(f32(*mine.shape[1:]),) * n_z,
        in_specs=[VMEM] * 2,
        out_specs=(VMEM,) * n_z,
        compiler_params=pltpu.CompilerParams(vmem_limit_bytes=SMALL),
        name="column_shares",
    )(mine, other)


def total(row_ref, col_refs):
    force = row_ref[0]
    for i in range(1, row_ref.shape[0]):
        force = force + row_ref[i]
    for ref in col_refs:
        force = force + ref[...]
    return force


def step_kernel(n_z, row_ref, *refs):
    col_refs = refs[:n_z]
    state_ref, u_ref, v_ref, spread_ref, now_ref, new_u_ref, new_v_ref = refs[n_z:]
    force = total(row_ref, col_refs)
    v = v_ref[...] + TIME_STEP * force
    u = u_ref[...] + TIME_STEP * v
    now = state_ref[3:6] + u
    new_u_ref[...] = u
    new_v_ref[...] = v
    now_ref[...] = now
    for i in range(spread_ref.shape[0]):
        spread_ref[i] = now


def next_step(row, cols, state, u, v):
    return pl.pallas_call(
        functools.partial(step_kernel, len(cols)),
        out_shape=(f32(*row.shape),) + (f32(*u.shape),) * 3,
        in_specs=[VMEM] * (4 + len(cols)),
        out_specs=(VMEM,) * 4,
        compiler_params=pltpu.CompilerParams(vmem_limit_bytes=SMALL),
        name="next_step",
    )(row, *cols, state, u, v)


def last_kernel(n_z, row_ref, *refs):
    col_refs = refs[:n_z]
    u_ref, v_ref, disp_ref, vel_ref = refs[n_z:]
    v = v_ref[...] + 0.5 * TIME_STEP * total(row_ref, col_refs)
    for c in range(3):
        for t in range(TILE_DEV):
            lanes = pl.ds(t * TILE, TILE)
            disp_ref[c:c + 1, lanes] = u_ref[c, t:t + 1, :]
            vel_ref[c:c + 1, lanes] = v[c, t:t + 1, :]


def last_step(row, cols, u, v):
    points = f32(3, TILE_DEV * TILE)
    return pl.pallas_call(
        functools.partial(last_kernel, len(cols)),
        out_shape=(points, points),
        in_specs=[VMEM] * (3 + len(cols)),
        out_specs=(VMEM,) * 2,
        compiler_params=pltpu.CompilerParams(vmem_limit_bytes=SMALL),
        name="last_half_step",
    )(row, *cols, u, v)


def to_sibling(x, n_row):
    return lax.ppermute(x, "row", [(i, i ^ 1) for i in range(n_row)])


def along_z(x, d, n_row):
    n_z = n_row // CORES
    return lax.ppermute(x, "row", [(i, (i // CORES + d) % n_z * CORES + i % CORES) for i in range(n_row)])


def swap(x):
    return lax.all_to_all(x, "col", 0, 0, tiled=True)


def column_gather(block, n_row):
    blocks = [block] + [along_z(block, d, n_row) for d in range(1, n_row // CORES)]
    return [x for mine in blocks for x in (mine, to_sibling(mine, n_row))][1:]


def column_sum(mine, sibling, n_row):
    parts = shares(mine, to_sibling(sibling, n_row))
    return [parts[0]] + [along_z(parts[d], d, n_row) for d in range(1, n_row // CORES)]


def per_device(
    rest_pos, displacement, velocity, accel_prev, material, moduli, pair_owner, pair_partner, pair_count, bond_mask, broken
):
    n_row, n_col = lax.axis_size("row"), lax.axis_size("col")
    spread, state, u, v, ids = start(
        n_col, moduli, pair_count, pair_owner.reshape(1, -1), pair_partner.reshape(1, -1),
        material.reshape(TILE_DEV, TILE), rest_pos, displacement, velocity, accel_prev
    )
    row, cols, states = swap(spread), column_gather(state, n_row), ()
    for step in range(STEPS):
        rowf, mine, sibling, *held = pair_forces(ids, row, cols, (bond_mask, broken), states)
        row_part = swap(rowf.reshape(n_col, 3, TILE_DEV, TILE))
        col_part = column_sum(mine, sibling, n_row)
        if step < STEPS - 1:
            spread, block, u, v = next_step(row_part, col_part, state, u, v)
            row, cols, states = swap(spread), column_gather(block, n_row), tuple(held)
    return last_step(row_part, col_part, u, v)


def solution(mesh):
    points, flat, masks = P(None, ("row", "col")), P(("row", "col")), P(("row", "col"), None, None)
    return jax.shard_map(
        per_device,
        mesh=mesh,
        in_specs=(points,) * 4 + (flat, P()) + (flat,) * 3 + (masks,) * 2,
        out_specs=(points, points),
        check_vma=False,
    )
```
